32 devices in a mesh: grp: 4 (over x, core), chan: 8 (over z, y).
Axes of the slice: x: 2, y: 2, z: 4, core: 2. Of those that a mesh axis runs over, the one named last changes fastest.
Arguments:
- vit_in: bfloat16 [4608, 1024], P(('grp', 'chan')), may hold values from -6 to 6
- hires: bfloat16 [8, 1536, 2304], P('grp', 'chan'), may hold values from -6 to 6
- size_class: int32 [8], P('grp'), may hold values from 24 to 48, as said below
- pool_mask: int32 [8, 2304], P('grp'), may hold values 0 or 1
- cotangent: bfloat16 [4608, 1024], P(('grp', 'chan')), may hold values from -6 to 6
- ln1_gain: bfloat16 [1024], P('chan'), may hold values from 0.5 to 1.5
- ln1_bias: bfloat16 [1024], P('chan'), may hold values from -1.75 to 1.75
- qkv_weight: bfloat16 [1024, 3072], P('chan'), may hold values from -0.1875 to 0.1875
- qv_bias: bfloat16 [2048], P('chan'), may hold values from -1.75 to 1.75
- out_weight: bfloat16 [1024, 1024], P('chan'), may hold values from -0.75 to 0.75
- out_bias: bfloat16 [1024], P('chan'), may hold values from -1.75 to 1.75
- ln2_gain: bfloat16 [1024], P('chan'), may hold values from 0.5 to 1.5
- ln2_bias: bfloat16 [1024], P('chan'), may hold values from -1.75 to 1.75
- fc1_weight: bfloat16 [1024, 4096], P('chan'), may hold values from -0.1875 to 0.1875
- fc1_bias: bfloat16 [4096], P('chan'), may hold values from -1.75 to 1.75
- fc2_weight: bfloat16 [4096, 1024], P('chan'), may hold values from -0.09375 to 0.09375
- fc2_bias: bfloat16 [1024], P('chan'), may hold values from -1.75 to 1.75
- dw7_weight: bfloat16 [49, 1536], P(None, 'chan'), may hold values from -0.875 to 0.875
- dw7_bias: bfloat16 [1536], P('chan'), may hold values from -1.75 to 1.75
- conv_gain: bfloat16 [1536], P('chan'), may hold values from 0.5 to 1.5
- conv_bias: bfloat16 [1536], P('chan'), may hold values from -1.75 to 1.75
- pw1_weight: bfloat16 [1536, 6144], P('chan'), may hold values from -0.15625 to 0.15625
- pw1_bias: bfloat16 [6144], P('chan'), may hold values from -1.75 to 1.75
- pw2_weight: bfloat16 [6144, 1536], P('chan'), may hold values from -0.078125 to 0.078125
- pw2_bias: bfloat16 [1536], P('chan'), may hold values from -1.75 to 1.75
- layer_scale: bfloat16 [1536], P('chan'), may hold values from 0.5 to 1.5
- proj_weight: bfloat16 [1536, 1024], P('chan'), may hold values from -0.15625 to 0.15625
- proj_bias: bfloat16 [1024], P('chan'), may hold values from -1.75 to 1.75
- dw3_weight: bfloat16 [9, 1024], P(None, 'chan'), may hold values from -2 to 2
- dw3_bias: bfloat16 [1024], P('chan'), may hold values from -1.75 to 1.75
- gate: bfloat16 [1024], P('chan'), may hold values from -1.5 to 1.5
Outputs:
- vit_out: float32 [4608, 1024], P(('grp', 'chan'))
- vit_grad: float32 [4608, 1024], P(('grp', 'chan'))
- hires_grad: float32 [8, 1536, 2304], P('grp', 'chan')
- grad_ln1_gain: float32 [1024], P('chan')
- grad_ln1_bias: float32 [1024], P('chan')
- grad_qkv_weight: float32 [1024, 3072], P('chan')
- grad_qv_bias: float32 [2048], P('chan')
- grad_out_weight: float32 [1024, 1024], P('chan')
- grad_out_bias: float32 [1024], P('chan')
- grad_ln2_gain: float32 [1024], P('chan')
- grad_ln2_bias: float32 [1024], P('chan')
- grad_fc1_weight: float32 [1024, 4096], P('chan')
- grad_fc1_bias: float32 [4096], P('chan')
- grad_fc2_weight: float32 [4096, 1024], P('chan')
- grad_fc2_bias: float32 [1024], P('chan')
- grad_dw7_weight: float32 [49, 1536], P(None, 'chan')
- grad_dw7_bias: float32 [1536], P('chan')
- grad_conv_gain: float32 [1536], P('chan')
- grad_conv_bias: float32 [1536], P('chan')
- grad_pw1_weight: float32 [1536, 6144], P('chan')
- grad_pw1_bias: float32 [6144], P('chan')
- grad_pw2_weight: float32 [6144, 1536], P('chan')
- grad_pw2_bias: float32 [1536], P('chan')
- grad_layer_scale: float32 [1536], P('chan')
- grad_proj_weight: float32 [1536, 1024], P('chan')
- grad_proj_bias: float32 [1024], P('chan')
- grad_dw3_weight: float32 [9, 1024], P(None, 'chan')
- grad_dw3_bias: float32 [1024], P('chan')
- grad_gate: float32 [1024], P('chan')
The draws below stay inside these ranges and needn't reach their ends.
Inputs may be any that keep to these rules, and one draw needn't show every extreme that they name: size_class[n] is 24, 32 or 48; every draw holds an image of each end value.
All inputs are finite; a program needn't handle non-finite values. No bound on the sum of `pool_mask` on one device may be relied on, other than what follows from the above.
Results may differ from the reference program's by a relative error of at most 0.022.
Values may be sent and summed in bfloat16 or wider, within the bound.
No kernel may reach another device: no remote copies, remote signals or barrier semaphores. Data moves between devices by JAX's collectives and lax.ppermute only.
A program may use at most 512 MiB of HBM per device.

```python
import jax
import jax.numpy as jnp
from jax import lax

D = 1024
HEADS = 16
HEAD_DIM = 64
MLP = 4096
CONV_WIDTH = 1536
CONV_MLP = 6144
KERNEL = 7
GRID = 24
IMG = 8
TOKENS = 4608
CELLS = 2304


def draw_size_class(key, part):
    drawn_index = jax.random.randint(key, (IMG,), 0, 3)
    shuffled = jax.random.permutation(jax.random.fold_in(key, 7), IMG)
    drawn_index = drawn_index.at[shuffled[0]].set(0)
    drawn_index = drawn_index.at[shuffled[1]].set(2)
    class_sides = jnp.array([GRID, 4 * GRID // 3, 2 * GRID], dtype=jnp.int32)
    return class_sides[drawn_index]


def plant(result, rng, low, high):
    extent = result.shape
    spot = [jax.random.randint(jax.random.fold_in(rng, axis), (), 0, extent[axis]) for axis in range(len(extent))]
    result = result.at[tuple(spot)].set(low)
    longest = extent.index(max(extent))
    spot[longest] = (spot[longest] + 1) % extent[longest]
    return result.at[tuple(spot)].set(high)


def steps_of(key, extent, cuts, low, top_value):
    level = 1.0
    for position, blocks in cuts:
        heights = jax.random.uniform(jax.random.fold_in(jax.random.fold_in(key, 6), position), (blocks,), jnp.float32, low / len(cuts), top_value / len(cuts))
        level = level * jnp.repeat(jnp.exp(heights), extent[position] // blocks).reshape((-1,) + (1,) * (len(extent) - 1 - position))
    return level


def scatter_about(rng, shape, deviation, bound, cuts=(), held_as=jnp.bfloat16):
    drawn = deviation * jax.random.normal(rng, shape, jnp.float32)
    if cuts:
        drawn = drawn * steps_of(rng, shape, cuts, -0.22, 0.18)
    return jnp.clip(drawn, -bound, bound).astype(held_as)


def setup_inputs(seed: int = 0) -> dict:
    keys = jax.random.split(jax.random.key(seed), 32)
    vit_in = scatter_about(keys[0], (TOKENS, D), 1.0, 6.0, ((0, 32),))
    hires = scatter_about(keys[1], (IMG, CONV_WIDTH, CELLS), 1.0, 6.0, ((0, 4), (1, 8)))
    size_class = draw_size_class(jax.random.fold_in(keys[31], 71), 0)
    pool_mask = plant((jax.random.randint(keys[3], (IMG, CELLS), 0, 8) < 7).astype(jnp.int32), jax.random.fold_in(keys[3], 1), 0, 1)
    cotangent = scatter_about(keys[4], (TOKENS, D), 1.0, 6.0, ((0, 32),))
    ln1_gain = jnp.clip(1.0 + 0.1 * jax.random.normal(keys[5], (D,), jnp.float32), 0.5, 1.5).astype(jnp.bfloat16)
    ln1_bias = scatter_about(keys[6], (D,), 0.3, 1.75, ((0, 8),))
    qkv_weight = scatter_about(keys[7], (D, 3 * D), D ** -0.5, 0.1875, ((0, 8),))
    qv_bias = scatter_about(keys[8], (2 * D,), 0.3, 1.75, ((0, 8),))
    out_weight = scatter_about(keys[9], (D, D), HEAD_DIM ** -0.5, 0.75, ((0, 8),))
    out_bias = scatter_about(keys[10], (D,), 0.3, 1.75, ((0, 8),))
    ln2_gain = jnp.clip(1.0 + 0.1 * jax.random.normal(keys[11], (D,), jnp.float32), 0.5, 1.5).astype(jnp.bfloat16)
    ln2_bias = scatter_about(keys[12], (D,), 0.3, 1.75, ((0, 8),))
    fc1_weight = scatter_about(keys[13], (D, MLP), D ** -0.5, 0.1875, ((0, 8),))
    fc1_bias = scatter_about(keys[14], (MLP,), 0.3, 1.75, ((0, 8),))
    fc2_weight = scatter_about(keys[15], (MLP, D), MLP ** -0.5, 0.09375, ((0, 8),))
    fc2_bias = scatter_about(keys[16], (D,), 0.3, 1.75, ((0, 8),))
    dw7_weight = scatter_about(keys[17], (KERNEL * KERNEL, CONV_WIDTH), (KERNEL * KERNEL) ** -0.5, 0.875, ((1, 8),))
    dw7_bias = scatter_about(keys[18], (CONV_WIDTH,), 0.3, 1.75, ((0, 8),))
    conv_gain = jnp.clip(1.0 + 0.1 * jax.random.normal(keys[19], (CONV_WIDTH,), jnp.float32), 0.5, 1.5).astype(jnp.bfloat16)
    conv_bias = scatter_about(keys[20], (CONV_WIDTH,), 0.3, 1.75, ((0, 8),))
    pw1_weight = scatter_about(keys[21], (CONV_WIDTH, CONV_MLP), CONV_WIDTH ** -0.5, 0.15625, ((0, 8),))
    pw1_bias = scatter_about(keys[22], (CONV_MLP,), 0.3, 1.75, ((0, 8),))
    pw2_weight = scatter_about(keys[23], (CONV_MLP, CONV_WIDTH), CONV_MLP ** -0.5, 0.078125, ((0, 8),))
    pw2_bias = scatter_about(keys[24], (CONV_WIDTH,), 0.3, 1.75, ((0, 8),))
    layer_scale = jnp.clip(1.0 + 0.1 * jax.random.normal(keys[25], (CONV_WIDTH,), jnp.float32), 0.5, 1.5).astype(jnp.bfloat16)
    proj_weight = scatter_about(keys[26], (CONV_WIDTH, D), CONV_WIDTH ** -0.5, 0.15625, ((0, 8),))
    proj_bias = scatter_about(keys[27], (D,), 0.3, 1.75, ((0, 8),))
    dw3_weight = scatter_about(keys[28], (9, D), 9 ** -0.5, 2.0, ((1, 8),))
    dw3_bias = scatter_about(keys[29], (D,), 0.3, 1.75, ((0, 8),))
    gate = jnp.clip(jax.random.uniform(keys[30], (D,), jnp.float32, -1.5, 1.5) * steps_of(keys[30], (D,), ((0, 8),), -0.4, 0.0), -1.5, 1.5).astype(jnp.bfloat16)
    return {"vit_in": vit_in, "hires": hires, "size_class": size_class, "pool_mask": pool_mask, "cotangent": cotangent, "ln1_gain": ln1_gain, "ln1_bias": ln1_bias, "qkv_weight": qkv_weight, "qv_bias": qv_bias, "out_weight": out_weight, "out_bias": out_bias, "ln2_gain": ln2_gain, "ln2_bias": ln2_bias, "fc1_weight": fc1_weight, "fc1_bias": fc1_bias, "fc2_weight": fc2_weight, "fc2_bias": fc2_bias, "dw7_weight": dw7_weight, "dw7_bias": dw7_bias, "conv_gain": conv_gain, "conv_bias": conv_bias, "pw1_weight": pw1_weight, "pw1_bias": pw1_bias, "pw2_weight": pw2_weight, "pw2_bias": pw2_bias, "layer_scale": layer_scale, "proj_weight": proj_weight, "proj_bias": proj_bias, "dw3_weight": dw3_weight, "dw3_bias": dw3_bias, "gate": gate}


@jax.custom_vjp
def low(v):
    return lax.optimization_barrier(v.astype(jnp.bfloat16)).astype(jnp.float32)

@jax.custom_vjp
def low_back(v):
    return v

def low_keep(v):
    return (low(v), None)

def low_pass(kept, grad):
    return (grad,)

def back_keep(v):
    return (v, None)

def back_low(kept, grad):
    return (low(grad),)
low.defvjp(low_keep, low_pass)
low_back.defvjp(back_keep, back_low)
HIGHEST = lax.Precision.HIGHEST
EPS_VIT = 1e-05
EPS_CONV = 1e-06

def product(left, right):
    return jnp.dot(left, right, precision=HIGHEST, preferred_element_type=jnp.float32)

def layer_norm(inputs, gain, shift_term, epsilon):
    mean_row = lax.optimization_barrier(jnp.mean(inputs, axis=-1, keepdims=True))
    centred = inputs - mean_row
    variance = lax.optimization_barrier(jnp.mean(centred * centred, axis=-1, keepdims=True))
    return centred * lax.rsqrt(variance + epsilon) * gain + shift_term

def branch_image(params, hires_image, map_size, mask_cells):
    map_side = 2 * GRID
    map_cells = map_side * map_side
    half_kernel = KERNEL // 2
    row_ids = lax.broadcasted_iota(jnp.int32, (map_side, map_side), 0).reshape(map_cells)
    col_ids = lax.broadcasted_iota(jnp.int32, (map_side, map_side), 1).reshape(map_cells)
    valid_cells = ((row_ids < map_size) & (col_ids < map_size)).astype(jnp.float32)
    masked_in = hires_image * valid_cells[None, :]
    framed = jnp.pad(masked_in.reshape(CONV_WIDTH, map_side, map_side), ((0, 0), (half_kernel, half_kernel), (half_kernel, half_kernel)))
    running = jnp.zeros((CONV_WIDTH, map_side, map_side), jnp.float32) + params['dw7_bias'][:, None, None]
    for row_step in range(KERNEL):
        for col_step in range(KERNEL):
            running = running + params['dw7_weight'][row_step * KERNEL + col_step][:, None, None] * framed[:, row_step:row_step + map_side, col_step:col_step + map_side]
    conv_out = running.reshape(CONV_WIDTH, map_cells) * valid_cells[None, :]
    conv_low = jnp.transpose(low_back(low(conv_out)))
    resid_in = jnp.transpose(low_back(masked_in))
    normed = low(layer_norm(conv_low, params['conv_gain'], params['conv_bias'], EPS_CONV))
    hidden = low_back(product(normed, params['pw1_weight']) + params['pw1_bias'])
    activ = low(jax.nn.gelu(hidden, approximate=False))
    branch_out = low_back(product(activ, params['pw2_weight']) + params['pw2_bias'])
    refined = low(resid_in + params['layer_scale'] * branch_out)
    cell_ids = lax.broadcasted_iota(jnp.int32, (map_cells,), 0)
    cell_row = cell_ids // map_side
    cell_col = cell_ids % map_side
    out_ids = lax.broadcasted_iota(jnp.int32, (GRID * GRID,), 0)
    out_row = out_ids // GRID
    out_col = out_ids % GRID
    row_hit = ((out_row * map_size // GRID)[:, None] <= cell_row[None, :]) & (cell_row[None, :] < (((out_row + 1) * map_size + GRID - 1) // GRID)[:, None])
    col_hit = ((out_col * map_size // GRID)[:, None] <= cell_col[None, :]) & (cell_col[None, :] < (((out_col + 1) * map_size + GRID - 1) // GRID)[:, None])
    pool_table = (row_hit & col_hit).astype(jnp.float32) * mask_cells.astype(jnp.float32)[None, :]
    pool_count = lax.optimization_barrier(jnp.sum(pool_table, axis=1))
    pooled = low(low_back(product(pool_table, refined) / jnp.maximum(pool_count, 1.0)[:, None]))
    adapt = low(low_back(product(pooled, params['proj_weight']) + params['proj_bias'])).reshape(GRID, GRID, D)
    framed_small = jnp.pad(adapt, ((1, 1), (1, 1), (0, 0)))
    running_small = jnp.zeros((GRID, GRID, D), jnp.float32) + params['dw3_bias']
    for row_step in range(3):
        for col_step in range(3):
            running_small = running_small + params['dw3_weight'][row_step * 3 + col_step] * framed_small[row_step:row_step + GRID, col_step:col_step + GRID]
    adapt_conv = low_back(running_small)
    return (jnp.tanh(params['gate']) * adapt_conv).reshape(GRID * GRID, D)

def attend(items):
    queries, key_rows, value_rows = items
    scores = low_back(jnp.einsum('qhd,khd->hqk', queries, key_rows, precision=HIGHEST) * HEAD_DIM ** (-0.5))
    probs = jax.nn.softmax(scores, axis=-1)
    context = jnp.einsum('hqk,khd->qhd', low(probs), value_rows, precision=HIGHEST)
    return low(low_back(context)).reshape(GRID * GRID, D)

def forward(params, vit_in, hires, size_class, pool_mask):
    checked = jax.checkpoint(branch_image)

    def one_image(items):
        return checked(params, items[0], items[1], items[2])
    adds = lax.map(one_image, (hires, size_class, pool_mask))
    mixed = vit_in + adds.reshape(TOKENS, D)
    norm1 = low(layer_norm(mixed, params['ln1_gain'], params['ln1_bias'], EPS_VIT))
    qv_full = params['qv_bias']
    bias_full = jnp.concatenate([qv_full[:D], jnp.zeros((D,), jnp.float32), qv_full[D:]])
    qkv = low(low_back(product(norm1, params['qkv_weight']) + bias_full))
    queries = qkv[:, :D].reshape(IMG, GRID * GRID, HEADS, HEAD_DIM)
    key_rows = qkv[:, D:2 * D].reshape(IMG, GRID * GRID, HEADS, HEAD_DIM)
    value_rows = qkv[:, 2 * D:].reshape(IMG, GRID * GRID, HEADS, HEAD_DIM)
    context = lax.map(jax.checkpoint(attend), (queries, key_rows, value_rows)).reshape(TOKENS, D)
    attn = low_back(product(context, params['out_weight']) + params['out_bias'])
    resid = mixed + attn
    norm2 = low(layer_norm(resid, params['ln2_gain'], params['ln2_bias'], EPS_VIT))
    hidden = low_back(product(norm2, params['fc1_weight']) + params['fc1_bias'])
    mlp_out = low_back(product(low(jax.nn.gelu(hidden, approximate=False)), params['fc2_weight']) + params['fc2_bias'])
    return resid + mlp_out

def reference(vit_in, hires, size_class, pool_mask, cotangent, ln1_gain, ln1_bias, qkv_weight, qv_bias, out_weight, out_bias, ln2_gain, ln2_bias, fc1_weight, fc1_bias, fc2_weight, fc2_bias, dw7_weight, dw7_bias, conv_gain, conv_bias, pw1_weight, pw1_bias, pw2_weight, pw2_bias, layer_scale, proj_weight, proj_bias, dw3_weight, dw3_bias, gate):
    params = dict(ln1_gain=ln1_gain.astype(jnp.float32), ln1_bias=ln1_bias.astype(jnp.float32), qkv_weight=qkv_weight.astype(jnp.float32), qv_bias=qv_bias.astype(jnp.float32), out_weight=out_weight.astype(jnp.float32), out_bias=out_bias.astype(jnp.float32), ln2_gain=ln2_gain.astype(jnp.float32), ln2_bias=ln2_bias.astype(jnp.float32), fc1_weight=fc1_weight.astype(jnp.float32), fc1_bias=fc1_bias.astype(jnp.float32), fc2_weight=fc2_weight.astype(jnp.float32), fc2_bias=fc2_bias.astype(jnp.float32), dw7_weight=dw7_weight.astype(jnp.float32), dw7_bias=dw7_bias.astype(jnp.float32), conv_gain=conv_gain.astype(jnp.float32), conv_bias=conv_bias.astype(jnp.float32), pw1_weight=pw1_weight.astype(jnp.float32), pw1_bias=pw1_bias.astype(jnp.float32), pw2_weight=pw2_weight.astype(jnp.float32), pw2_bias=pw2_bias.astype(jnp.float32), layer_scale=layer_scale.astype(jnp.float32), proj_weight=proj_weight.astype(jnp.float32), proj_bias=proj_bias.astype(jnp.float32), dw3_weight=dw3_weight.astype(jnp.float32), dw3_bias=dw3_bias.astype(jnp.float32), gate=gate.astype(jnp.float32))

    def wrapped(weights, tokens, maps):
        return forward(weights, tokens, maps, size_class, pool_mask)
    primal, pullback = jax.vjp(wrapped, params, vit_in.astype(jnp.float32), hires.astype(jnp.float32))
    grads, vit_grad, hires_grad = pullback(cotangent.astype(jnp.float32))
    return (primal, vit_grad, hires_grad, grads['ln1_gain'], grads['ln1_bias'], grads['qkv_weight'], grads['qv_bias'], grads['out_weight'], grads['out_bias'], grads['ln2_gain'], grads['ln2_bias'], grads['fc1_weight'], grads['fc1_bias'], grads['fc2_weight'], grads['fc2_bias'], grads['dw7_weight'], grads['dw7_bias'], grads['conv_gain'], grads['conv_bias'], grads['pw1_weight'], grads['pw1_bias'], grads['pw2_weight'], grads['pw2_bias'], grads['layer_scale'], grads['proj_weight'], grads['proj_bias'], grads['dw3_weight'], grads['dw3_bias'], grads['gate'])
```

```python
from functools import partial
from types import SimpleNamespace
from typing import Any, NamedTuple

import jax
import jax.numpy as jnp
from jax import lax
from jax.experimental import pallas as pl
from jax.experimental.pallas import tpu as pltpu
from jax.sharding import PartitionSpec as P

D = 1024
HEADS = 16
HEAD_DIM = 64
KERNEL = 7
GRID = 24
BANDS = 4
SIDE = 2 * GRID
CELLS = SIDE * SIDE
BAND_CELLS = CELLS // BANDS
ROWS = GRID // BANDS
TOKENS = ROWS * GRID
PAIR = 1

EPS_VIT = 1e-05
EPS_CONV = 1e-06

CHAN = "chan"
GRP = "grp"

f32 = jnp.float32
bf16 = jnp.bfloat16


def flip(value, axis, bit):
    return lax.ppermute(value, axis, [(i, i ^ (1 << bit)) for i in range(lax.axis_size(axis))])


def bit_at(axis, bit):
    return (lax.axis_index(axis) >> bit) & 1


def shifted(value, axis, steps):
    count = lax.axis_size(axis)
    first, last = (max(0, -steps), min(count, count - steps))
    return lax.ppermute(value, axis, [(source, source + steps) for source in range(first, last)])


def count_bits(axis):
    return lax.axis_size(axis).bit_length() - 1


def reorder(pieces, axis=GRP):
    for bit in range(count_bits(axis)):
        swap = bit_at(axis, bit) == 1
        pieces = [
            jnp.where(swap, pieces[place ^ (1 << bit)], pieces[place])
            for place in range(len(pieces))
        ]
    return pieces


def chan_merge(own, got, bit):
    upper = bit_at(CHAN, bit) == 1
    both = jnp.stack([jnp.where(upper, got, own), jnp.where(upper, own, got)], axis=1)
    return both.reshape((2 * own.shape[0],) + own.shape[1:])


def gather(block, plan):
    pieces = {0: block[None]}
    for axis, bit in plan:
        got = yield {place: flip(piece, axis, bit) for place, piece in pieces.items()}
        if axis == CHAN:
            pieces = {place: chan_merge(pieces[place], got[place], bit) for place in pieces}
        else:
            pieces.update({place ^ (1 << bit): piece for place, piece in got.items()})
    return {
        place: piece.reshape((-1,) + piece.shape[2:]) for place, piece in sorted(pieces.items())
    }


def flip_crosswise(value, swapped):
    groups, parts = lax.axis_size(GRP), lax.axis_size(CHAN)
    pairs = []
    for member in range(groups):
        for place in range(parts):
            other = (member, place ^ 1) if member % 2 == swapped else (member ^ 1 << PAIR, place)
            pairs.append((member * parts + place, other[0] * parts + other[1]))
    return lax.ppermute(value, (GRP, CHAN), pairs)


def gather_crosswise(block, plan):
    own = block[None]
    for axis, bit in plan:
        if axis == CHAN and bit > 0:
            got = yield flip(own, axis, bit)
            own = chan_merge(own, got, bit)
    first = yield flip_crosswise(own, 0)
    second = yield (flip_crosswise(own, 1), flip_crosswise(first, 1))
    even = lax.axis_index(GRP) % 2 == 0
    beside = jnp.where(even, first, second[0])
    across = jnp.where(even, second[0], first)
    pieces = {0: chan_merge(own, beside, 0), 1 << PAIR: chan_merge(across, second[1], 0)}
    for axis, bit in plan:
        if axis == GRP and bit != PAIR:
            got = yield {place: flip(piece, axis, bit) for place, piece in pieces.items()}
            pieces.update({place ^ (1 << bit): piece for place, piece in got.items()})
    return {
        place: piece.reshape((-1,) + piece.shape[2:]) for place, piece in sorted(pieces.items())
    }


class Flow:
    def __init__(self, steps):
        self.steps = steps
        self.pending = next(steps)
        self.result = None

    def advance(self, got):
        try:
            self.pending = self.steps.send(got)
        except StopIteration as stop:
            self.pending, self.result = None, stop.value

    def finish(self):
        while self.pending is not None:
            self.advance(self.pending)
        return self.result


def sync(value, *flows):
    flows = [flow for flow in flows if flow.pending is not None]
    value, arrived = lax.optimization_barrier((value, [flow.pending for flow in flows]))
    for flow, got in zip(flows, arrived):
        flow.advance(got)
    return value


def added(left, right):
    return (left.astype(f32) + right.astype(f32)).astype(left.dtype)


def scatter_sum(pieces, plan):
    parts = lax.axis_size(CHAN)
    pieces = {
        place: piece.reshape((parts, piece.shape[0] // parts) + piece.shape[1:])
        for place, piece in pieces.items()
    }
    for axis, bit in reversed(plan):
        if axis == CHAN:
            mine = bit_at(CHAN, bit)
            kept, sent = {}, {}
            for place, piece in pieces.items():
                halves = piece.reshape((piece.shape[0] // 2, 2) + piece.shape[1:])
                kept[place] = lax.dynamic_index_in_dim(halves, mine, 1, keepdims=False)
                sent[place] = lax.dynamic_index_in_dim(halves, 1 - mine, 1, keepdims=False)
        else:
            kept = {place: piece for place, piece in pieces.items() if not place >> bit & 1}
            sent = {place: pieces[place ^ (1 << bit)] for place in kept}
        got = yield {place: flip(piece, axis, bit) for place, piece in sent.items()}
        pieces = {place: added(kept[place], got[place]) for place in kept}
    return pieces[0][0]


def halve(piece, bit):
    mine = bit_at(CHAN, bit)
    halves = piece.reshape((piece.shape[0] // 2, 2) + piece.shape[1:])
    return [lax.dynamic_index_in_dim(halves, i, 1, keepdims=False) for i in (mine, 1 - mine)]


def crosswise_sum(pieces, plan):
    parts = lax.axis_size(CHAN)
    pieces = {
        place: piece.reshape((parts, piece.shape[0] // parts) + piece.shape[1:])
        for place, piece in pieces.items()
    }
    for axis, bit in reversed(plan):
        if axis == GRP and bit != PAIR:
            kept = {place: piece for place, piece in pieces.items() if not place >> bit & 1}
            sent = {place: pieces[place ^ (1 << bit)] for place in kept}
            got = yield {place: flip(piece, axis, bit) for place, piece in sent.items()}
            pieces = {place: added(kept[place], got[place]) for place in kept}
    even = lax.axis_index(GRP) % 2 == 0
    own, beside = halve(pieces[0], 0)
    across, far = halve(pieces[1 << PAIR], 0)
    got = yield (
        flip_crosswise(jnp.where(even, across, beside), 1),
        flip_crosswise(far, 1),
    )
    own = added(own, got[0])
    other = added(jnp.where(even, beside, across), got[1])
    got = yield flip_crosswise(other, 0)
    own = added(own, got)
    for axis, bit in reversed(plan):
        if axis == CHAN and bit > 0:
            kept, sent = halve(own, bit)
            got = yield flip(sent, axis, bit)
            own = added(kept, got)
    return own[0]


def scatter_and_spread(pieces, plan, sums=scatter_sum):
    block = yield from sums(pieces, plan)
    pieces = {0: lax.optimization_barrier(block)}
    for bit in reversed(range(count_bits(GRP))):
        got = yield {place: flip(piece, GRP, bit) for place, piece in pieces.items()}
        pieces.update({place ^ (1 << bit): piece for place, piece in got.items()})
    return [pieces[place] for place in range(len(pieces))]


def total_sum(bundle, plan):
    total = yield from scatter_sum({0: bundle}, [step for step in plan if step[0] == CHAN])
    for axis, bit in plan:
        if axis == GRP:
            got = yield flip(total, axis, bit)
            total = total + got
    return total


def my_part(value, dim):
    return lax.dynamic_index_in_dim(value, lax.axis_index(GRP), dim, keepdims=False)


def pick(pieces, index):
    for bit in range(len(pieces).bit_length() - 1):
        odd = (index >> bit) & 1 == 1
        pieces = [
            jnp.where(odd, pieces[2 * i + 1], pieces[2 * i]) for i in range(len(pieces) // 2)
        ]
    return pieces[0]


def band_exchange(pieces):
    band = lax.axis_index(CHAN) % BANDS
    count = lax.axis_size(CHAN)
    received = [pick(pieces, band)]
    for apart in range(1, BANDS):
        sent = pick(pieces, band ^ apart)
        received.append(lax.ppermute(sent, CHAN, [(i, i ^ apart) for i in range(count)]))
    return received


def band_return(received):
    band = lax.axis_index(CHAN) % BANDS
    count = lax.axis_size(CHAN)
    back = [received[0]]
    for apart in range(1, BANDS):
        back.append(lax.ppermute(received[apart], CHAN, [(i, i ^ apart) for i in range(count)]))
    return [pick(back, place ^ band) for place in range(BANDS)]


def all_to_all(value):
    return lax.all_to_all(value, CHAN, split_axis=0, concat_axis=0, tiled=True)


def layer_norm(inputs, gain, shift_term, epsilon):
    mean_row = jnp.mean(inputs, axis=-1, keepdims=True)
    centred = inputs - mean_row
    variance = jnp.mean(centred * centred, axis=-1, keepdims=True)
    return centred * lax.rsqrt(variance + epsilon) * gain + shift_term


def norm_vit(inputs, gain, shift_term):
    return layer_norm(inputs, gain, shift_term, EPS_VIT)


def gelu_and_slope(inputs):
    below = 0.5 * (1.0 + lax.erf(inputs * (0.5**0.5)))
    slope = below + inputs * jnp.exp(-0.5 * inputs * inputs) * 0.3989422804014327
    return (inputs * below).astype(bf16), slope.astype(bf16)


def matmul(left, right):
    return jnp.dot(left, right, preferred_element_type=f32)


def left_grad(inputs, grads):
    return lax.dot_general(
        inputs, grads, (((0,), (0,)), ((), ())), preferred_element_type=f32
    ).astype(bf16)


def right_grad(grads, weight):
    return lax.dot_general(grads, weight, (((1,), (1,)), ((), ())), preferred_element_type=f32)


def column_sum(grads):
    return jnp.sum(grads.astype(f32), axis=0)


PITCH = SIDE + 8
HALF = KERNEL // 2
FRAME = (SIDE + 2 * HALF) * PITCH + 8
LANES = 128


def frame_at(row, col):
    return pl.multiple_of((row + HALF) * PITCH, 8) + 8 + col


def valid_row(row, sizes):
    cols = lax.broadcasted_iota(jnp.int32, (SIDE, LANES), 0)
    return jnp.where(row < sizes, cols, SIDE) < sizes


def whole(*shape):
    return pl.BlockSpec(shape, lambda *grid: (0,) * len(shape))


def in_smem():
    return pl.BlockSpec(memory_space=pltpu.SMEM)


def band_rows(step, band):
    return pl.ds(pl.multiple_of(step * band, 16), BAND_CELLS)


def convolve_tiles(sizes_ref, taps_ref, bias_ref, maps_ref, cells_ref, masked_ref, turned, framed, first=0):
    framed[...] = jnp.zeros_like(framed)
    for lane in range(0, maps_ref.shape[0], LANES):
        here = slice(first + lane, first + lane + LANES)
        for begin in range(0, CELLS, LANES):
            columns = maps_ref[lane : lane + LANES, begin : begin + LANES]
            turned[begin : begin + LANES] = columns.astype(f32).T
        sizes = sizes_ref[:, here]

        def fill(row, carry):
            cells = pl.ds(pl.multiple_of(row * SIDE, 16), SIDE)
            inner = jnp.where(valid_row(row, sizes), turned[cells], 0.0)
            framed[pl.ds(frame_at(row, 0), SIDE)] = inner
            masked_ref[cells, here] = inner.astype(bf16)
            return carry

        lax.fori_loop(0, SIDE, fill, 0)

        def convolve(row, carry):
            total = jnp.zeros((SIDE, LANES), f32) + bias_ref[:, here]
            for row_step in range(KERNEL):
                for col_step in range(KERNEL):
                    tap = row_step * KERNEL + col_step
                    total = total + taps_ref[tap : tap + 1, here] * framed[
                        pl.ds(frame_at(row + row_step - HALF, col_step - HALF), SIDE)
                    ]
            cells = pl.ds(pl.multiple_of(row * SIDE, 16), SIDE)
            cells_ref[cells, here] = jnp.where(valid_row(row, sizes), total, 0.0).astype(bf16)
            return carry

        lax.fori_loop(0, SIDE, convolve, 0)


def conv_forward_kernel(sizes_ref, taps_ref, bias_ref, maps_ref, cells_ref, masked_ref, turned, framed):
    convolve_tiles(sizes_ref, taps_ref, bias_ref, maps_ref, cells_ref, masked_ref, turned, framed)


def conv_forward_last_kernel(
    step_ref,
    sizes_ref,
    taps_ref,
    bias_ref,
    maps_ref,
    early_cells_ref,
    early_masked_ref,
    conv_ref,
    bands_ref,
    masked_ref,
    turned,
    framed,
    cells_ref,
):
    early, channels = early_cells_ref.shape[1], conv_ref.shape[2]
    cells_ref[:, :early] = early_cells_ref[...]
    masked_ref[:, :early] = early_masked_ref[...]
    convolve_tiles(
        sizes_ref, taps_ref, bias_ref, maps_ref, cells_ref, masked_ref, turned, framed, early
    )
    for image in range(masked_ref.shape[1] // channels):
        here = slice(image * channels, (image + 1) * channels)
        for band in range(BANDS):
            rows = band_rows(step_ref[image], band)
            conv_ref[image * BANDS + band] = cells_ref[rows, here]
            bands_ref[image * BANDS + band] = masked_ref[rows, here]


def conv_backward_kernel(
    step_ref,
    sizes_ref,
    taps_ref,
    masked_ref,
    grad_ref,
    resid_ref,
    *refs,
    first,
):
    (
        out_ref,
        tap_grad_ref,
        framed,
        framed_grad,
        field,
        sums,
        grad_cells,
        resid_cells,
    ) = refs[-8:]
    lanes, channels = masked_ref.shape[1], grad_ref.shape[2]
    framed[...] = jnp.zeros_like(framed)
    framed_grad[...] = jnp.zeros_like(framed_grad)
    grad_cells[...] = jnp.zeros_like(grad_cells)
    resid_cells[...] = jnp.zeros_like(resid_cells)
    for image in range(lanes // channels):
        here = slice(image * channels, (image + 1) * channels)
        for band in range(BANDS):
            rows = band_rows(step_ref[image], band)
            grad_cells[rows, here] = grad_ref[image * BANDS + band]
            resid_cells[rows, here] = resid_ref[image * BANDS + band]

    def in_eights(value):
        return jnp.sum(value.reshape(SIDE // 8, 8, LANES), axis=0)

    for tile in range(0, out_ref.shape[0], LANES):
        here = slice(first + tile, first + tile + LANES)
        block = slice(tile, tile + LANES)
        sums[...] = jnp.zeros_like(sums)
        sizes = sizes_ref[:, here]

        def fill(row, carry):
            cells = pl.ds(pl.multiple_of(row * SIDE, 16), SIDE)
            framed[pl.ds(frame_at(row, 0), SIDE)] = masked_ref[cells, here].astype(f32)
            grads = jnp.where(valid_row(row, sizes), grad_cells[cells, here].astype(f32), 0.0)
            framed_grad[pl.ds(frame_at(row, 0), SIDE)] = grads
            return carry

        lax.fori_loop(0, SIDE, fill, 0)

        def convolve(row, carry):
            cells = pl.ds(pl.multiple_of(row * SIDE, 16), SIDE)
            total = resid_cells[cells, here].astype(f32)
            grads = framed_grad[pl.ds(frame_at(row, 0), SIDE)]
            for row_step in range(KERNEL):
                for col_step in range(KERNEL):
                    tap = row_step * KERNEL + col_step
                    total = total + taps_ref[tap : tap + 1, here] * framed_grad[
                        pl.ds(frame_at(row + HALF - row_step, HALF - col_step), SIDE)
                    ]
                    shifted_in = framed[
                        pl.ds(frame_at(row + row_step - HALF, col_step - HALF), SIDE)
                    ]
                    sums[tap * 8 : tap * 8 + 8] += in_eights(grads * shifted_in)
            last = KERNEL * KERNEL * 8
            sums[last : last + 8] += in_eights(grads)
            field[cells] = jnp.where(valid_row(row, sizes), total, 0.0)
            return carry

        lax.fori_loop(0, SIDE, convolve, 0)
        for begin in range(0, CELLS, LANES):
            out_ref[block, begin : begin + LANES] = field[begin : begin + LANES].T
        for tap in range(KERNEL * KERNEL + 1):
            tap_grad_ref[tap : tap + 1, block] = jnp.sum(
                sums[tap * 8 : tap * 8 + 8], axis=0, keepdims=True
            )


def kernel_call(kernel, name, in_specs, out_shape, scratch_shapes=(), vmem=40):
    return pl.pallas_call(
        kernel,
        grid=(1,),
        in_specs=in_specs,
        out_specs=[whole(*out.shape) for out in out_shape],
        out_shape=out_shape,
        scratch_shapes=list(scratch_shapes),
        compiler_params=pltpu.CompilerParams(vmem_limit_bytes=vmem << 20),
        name=name,
    )


def conv_forward(hires, size_class, taps, bias, between):
    images, channels = hires.shape[:2]
    lanes = images * channels
    maps = hires.reshape(lanes, CELLS)
    sizes = jnp.repeat(size_class, channels)[None]
    lane_taps = jnp.tile(taps.astype(f32), (1, images))
    lane_bias = jnp.tile(bias.astype(f32)[None], (1, images))
    steps = size_class // BANDS * SIDE
    early = max(1, lanes // LANES * 2 // 3) * LANES
    bands = jax.ShapeDtypeStruct((images * BANDS, BAND_CELLS, channels), bf16)
    cells = jax.ShapeDtypeStruct((CELLS, lanes), bf16)
    early_cells = jax.ShapeDtypeStruct((CELLS, early), bf16)
    vectors = [whole(1, lanes), whole(KERNEL * KERNEL, lanes), whole(1, lanes)]
    scratch = [pltpu.VMEM((CELLS, LANES), f32), pltpu.VMEM((FRAME, LANES), f32)]
    given = (sizes, lane_taps, lane_bias)
    done = kernel_call(
        conv_forward_kernel,
        "depthwise_forward",
        vectors + [whole(early, CELLS)],
        [early_cells, early_cells],
        scratch,
    )(*given, maps)
    late = lanes - early
    late_maps = pl.BlockSpec((late, CELLS), lambda i: (early // late, 0))
    conv, masked_bands, masked = kernel_call(
        conv_forward_last_kernel,
        "depthwise_forward_last",
        [in_smem()] + vectors + [late_maps, whole(CELLS, early), whole(CELLS, early)],
        [bands, bands, cells],
        scratch + [pltpu.VMEM((CELLS, lanes), bf16)],
    )(steps, *given, maps, *between(done))
    return conv, masked_bands, (steps, sizes, lane_taps, masked)


def conv_backward(saved, grad_bands, resid_bands, between):
    steps, sizes, lane_taps, masked = saved
    images, lanes, taps = steps.shape[0], sizes.shape[1], KERNEL * KERNEL
    early = max(1, lanes // LANES * 2 // 3) * LANES
    args = [steps, sizes, lane_taps, masked, grad_bands, resid_bands]
    specs = [in_smem(), whole(1, lanes), whole(taps, lanes), whole(CELLS, lanes)]
    specs += [whole(*grad_bands.shape), whole(*resid_bands.shape)]
    tap_grads = []
    for first, count in ((0, early), (early, lanes - early)):
        index = first // count
        field, tap_grad = pl.pallas_call(
            partial(conv_backward_kernel, first=first),
            grid=(1,),
            in_specs=specs,
            out_specs=[
                pl.BlockSpec((count, CELLS), lambda i, index=index: (index, 0)),
                whole(taps + 1, count),
            ],
            out_shape=[
                jax.ShapeDtypeStruct((lanes, CELLS), f32),
                jax.ShapeDtypeStruct((taps + 1, count), f32),
            ],
            input_output_aliases={6: 0} if first else {},
            scratch_shapes=[
                pltpu.VMEM((FRAME, LANES), f32),
                pltpu.VMEM((FRAME, LANES), f32),
                pltpu.VMEM((CELLS, LANES), f32),
                pltpu.VMEM(((taps + 1) * 8, LANES), f32),
                pltpu.VMEM((CELLS, lanes), bf16),
                pltpu.VMEM((CELLS, lanes), bf16),
            ],
            compiler_params=pltpu.CompilerParams(vmem_limit_bytes=40 << 20),
            name="depthwise_backward",
        )(*args)
        tap_grads.append(tap_grad)
        if not first:
            field = between(field)
            args.append(field)
            specs = specs + [pl.BlockSpec(memory_space=pl.ANY)]
    tap_grads = jnp.concatenate(tap_grads, axis=1).reshape(taps + 1, images, -1)
    return field.reshape(images, -1, CELLS), jnp.sum(tap_grads, axis=1)


def shape_of(dtype, *shape):
    return jax.ShapeDtypeStruct(shape, dtype)


def blocks_of(arrays):
    return [whole(*array.shape) for array in arrays]


def split_rows(count):
    return next(rows for rows in (96, 64, 48, 32, 16) if count % rows == 0)


def conv_norm_kernel(blocks_ref, gain_ref, bias_ref, out_ref):
    parts, rows, channels = blocks_ref.shape
    width = parts * channels
    blocks = [blocks_ref[part].astype(f32) for part in range(parts)]
    mean = sum(jnp.sum(block, axis=1, keepdims=True) for block in blocks) / width
    blocks = [block - mean for block in blocks]
    variance = sum(jnp.sum(block * block, axis=1, keepdims=True) for block in blocks) / width
    scale = lax.rsqrt(variance + EPS_CONV)
    for part in range(parts):
        here = slice(part * channels, (part + 1) * channels)
        normed = blocks[part] * scale * gain_ref[:, here] + bias_ref[:, here]
        out_ref[:, here] = normed.astype(bf16)


def conv_norm_forward(blocks, gain, bias):
    parts, cells, channels = blocks.shape
    width, rows = parts * channels, split_rows(cells)
    return pl.pallas_call(
        conv_norm_kernel,
        grid=(cells // rows,),
        in_specs=[
            pl.BlockSpec((parts, rows, channels), lambda i: (0, i, 0)),
            whole(1, width),
            whole(1, width),
        ],
        out_specs=pl.BlockSpec((rows, width), lambda i: (i, 0)),
        out_shape=shape_of(bf16, cells, width),
        compiler_params=pltpu.CompilerParams(vmem_limit_bytes=32 << 20),
        name="conv_norm_forward",
    )(blocks, gain[None], bias[None])


def conv_norm_grad_kernel(blocks_ref, gain_ref, own_ref, other_ref, out_ref, sums_ref):
    parts, rows, channels = blocks_ref.shape
    width = parts * channels

    @pl.when(pl.program_id(0) == 0)
    def _():
        sums_ref[...] = jnp.zeros_like(sums_ref)

    blocks = [blocks_ref[part].astype(f32) for part in range(parts)]
    mean = sum(jnp.sum(block, axis=1, keepdims=True) for block in blocks) / width
    blocks = [block - mean for block in blocks]
    variance = sum(jnp.sum(block * block, axis=1, keepdims=True) for block in blocks) / width
    scale = lax.rsqrt(variance + EPS_CONV)
    grads, mean_grad, mean_both = [], 0.0, 0.0
    for part in range(parts):
        here = slice(part * channels, (part + 1) * channels)
        grad = own_ref[:, here].astype(f32) + other_ref[:, here].astype(f32)
        blocks[part] = blocks[part] * scale
        both = grad * blocks[part]
        sums_ref[0:1, here] += jnp.sum(both, axis=0, keepdims=True)
        sums_ref[1:2, here] += jnp.sum(grad, axis=0, keepdims=True)
        grads.append(grad * gain_ref[:, here])
        mean_grad += jnp.sum(grads[part], axis=1, keepdims=True)
        mean_both += jnp.sum(grads[part] * blocks[part], axis=1, keepdims=True)
    for part in range(parts):
        value = grads[part] - mean_grad / width - blocks[part] * (mean_both / width)
        out_ref[part] = (scale * value).astype(bf16)


def conv_norm_backward(blocks, gain, own, other):
    parts, cells, channels = blocks.shape
    width, rows = parts * channels, split_rows(cells)
    return pl.pallas_call(
        conv_norm_grad_kernel,
        grid=(cells // rows,),
        in_specs=[
            pl.BlockSpec((parts, rows, channels), lambda i: (0, i, 0)),
            whole(1, width),
            pl.BlockSpec((rows, width), lambda i: (i, 0)),
            pl.BlockSpec((rows, width), lambda i: (i, 0)),
        ],
        out_specs=[
            pl.BlockSpec((parts, rows, channels), lambda i: (0, i, 0)),
            whole(2, width),
        ],
        out_shape=[shape_of(bf16, parts, cells, channels), shape_of(f32, 2, width)],
        compiler_params=pltpu.CompilerParams(vmem_limit_bytes=32 << 20),
        name="conv_norm_backward",
    )(blocks, gain[None], own, other)


def dot_nt(left, right):
    return lax.dot_general(left, right, (((1,), (1,)), ((), ())), preferred_element_type=f32)


def dot_tn(left, right):
    return lax.dot_general(left, right, (((0,), (0,)), ((), ())), preferred_element_type=f32)


def head_parts(joined, head, share):
    return [
        joined[:, kind * share + head * HEAD_DIM : kind * share + (head + 1) * HEAD_DIM]
        for kind in range(3)
    ]


def softmax_rows(queries, keys):
    scores = dot_nt(queries, keys) * HEAD_DIM ** (-0.5)
    weights = jnp.exp(scores - jnp.max(scores, axis=1, keepdims=True))
    return weights / jnp.sum(weights, axis=1, keepdims=True)


def attention_kernel(*refs):
    inputs, (context_ref, joined_ref) = refs[:BANDS], refs[BANDS:]
    for band in range(BANDS):
        joined_ref[band * TOKENS : (band + 1) * TOKENS] = inputs[band][...]
    share = context_ref.shape[2]
    for head in range(share // HEAD_DIM):
        queries, keys, values = head_parts(joined_ref, head, share)
        probs = softmax_rows(queries, keys).astype(bf16)
        context = jnp.dot(probs, values, preferred_element_type=f32).astype(bf16)
        for band in range(BANDS):
            context_ref[band, :, head * HEAD_DIM : (head + 1) * HEAD_DIM] = context[
                band * TOKENS : (band + 1) * TOKENS
            ]


def attention(pieces):
    share = pieces[0].shape[1] // 3
    return kernel_call(
        attention_kernel,
        "attention_forward",
        blocks_of(pieces),
        [shape_of(bf16, BANDS, TOKENS, share), shape_of(bf16, BANDS * TOKENS, 3 * share)],
    )(*pieces)


def attention_grad_kernel(joined_ref, *refs):
    inputs, (out_ref, grad_ref, result) = refs[:BANDS], refs[BANDS:]
    for band in range(BANDS):
        grad_ref[band * TOKENS : (band + 1) * TOKENS] = inputs[band][...]
    share = grad_ref.shape[1]
    for head in range(share // HEAD_DIM):
        queries, keys, values = head_parts(joined_ref, head, share)
        grads = grad_ref[:, head * HEAD_DIM : (head + 1) * HEAD_DIM]
        probs = softmax_rows(queries, keys)
        grad_probs = dot_nt(grads, values)
        row_dot = jnp.sum(probs * grad_probs, axis=1, keepdims=True)
        grad_scores = (probs * (grad_probs - row_dot)).astype(bf16)
        scale = HEAD_DIM ** (-0.5)
        parts = (
            jnp.dot(grad_scores, keys, preferred_element_type=f32) * scale,
            dot_tn(grad_scores, queries) * scale,
            dot_tn(probs.astype(bf16), grads),
        )
        for kind, part in enumerate(parts):
            begin = kind * share + head * HEAD_DIM
            result[:, begin : begin + HEAD_DIM] = part.astype(bf16)
    for band in range(BANDS):
        out_ref[band] = result[band * TOKENS : (band + 1) * TOKENS]


def attention_grad(joined, pieces):
    share = pieces[0].shape[1]
    return kernel_call(
        attention_grad_kernel,
        "attention_backward",
        [whole(*joined.shape)] + blocks_of(pieces),
        [shape_of(bf16, BANDS, TOKENS, 3 * share)],
        [
            pltpu.VMEM((BANDS * TOKENS, share), bf16),
            pltpu.VMEM((BANDS * TOKENS, 3 * share), bf16),
        ],
    )(joined, *pieces)[0]


GRID_PITCH = GRID + 8
GRID_FRAME = (ROWS + 2) * GRID_PITCH + 8


def fill_frame(frame_ref, keep_ref, before_ref, inner_ref, after_ref):
    frame_ref[...] = jnp.zeros_like(frame_ref)
    inner = inner_ref[...].astype(f32)
    rows = [before_ref[...].astype(f32) * keep_ref[0].astype(f32)]
    rows += [inner[row * GRID : (row + 1) * GRID] for row in range(ROWS)]
    rows += [after_ref[...].astype(f32) * keep_ref[1].astype(f32)]
    for row, value in enumerate(rows):
        begin = row * GRID_PITCH + 8
        frame_ref[begin : begin + GRID] = value


def frame_row(frame_ref, row, col):
    begin = row * GRID_PITCH + 8 + col
    return frame_ref[begin : begin + GRID]


def vit_norm(value):
    mean = jnp.mean(value, axis=1, keepdims=True)
    centred = value - mean
    variance = jnp.mean(centred * centred, axis=1, keepdims=True)
    scale = lax.rsqrt(variance + EPS_VIT)
    return centred * scale, scale


def mix_kernel(
    keep_ref, before_ref, inner_ref, after_ref, taps_ref, vectors_ref, vit_ref, adapt_ref, mixed_ref, norm_ref, frame
):
    fill_frame(frame, keep_ref, before_ref, inner_ref, after_ref)
    bias, gate_tanh, gain, shift = (vectors_ref[i : i + 1] for i in range(4))
    for row in range(ROWS):
        total = jnp.zeros((GRID, D), f32) + bias
        for row_step in range(3):
            for col_step in range(3):
                tap = row_step * 3 + col_step
                total = total + taps_ref[tap : tap + 1] * frame_row(
                    frame, row + row_step, col_step - 1
                )
        adapt_ref[row * GRID : (row + 1) * GRID] = total
    mixed = vit_ref[...].astype(f32) + gate_tanh * adapt_ref[...]
    mixed_ref[...] = mixed
    norm_ref[...] = (vit_norm(mixed)[0] * gain + shift).astype(bf16)


def mix_forward(keep, before, inner, after, taps, vectors, vit_in):
    return kernel_call(
        mix_kernel,
        "mix_forward",
        [in_smem()] + blocks_of((before, inner, after, taps, vectors, vit_in)),
        [shape_of(f32, TOKENS, D), shape_of(f32, TOKENS, D), shape_of(bf16, TOKENS, D)],
        [pltpu.VMEM((GRID_FRAME, D), f32)],
    )(keep, before, inner, after, taps, vectors, vit_in)


def norm_grad(value, gain, grad):
    xhat, scale = vit_norm(value)
    gained = grad * gain
    back = (
        gained
        - jnp.mean(gained, axis=1, keepdims=True)
        - xhat * jnp.mean(gained * xhat, axis=1, keepdims=True)
    )
    return (
        scale * back,
        jnp.sum(grad * xhat, axis=0, keepdims=True),
        jnp.sum(grad, axis=0, keepdims=True),
    )


def mix_grad_kernel(vectors_ref, grad_ref, mixed_ref, resid_ref, adapt_ref, out_ref, low_ref, sums_ref):
    gate_tanh, gain = vectors_ref[1:2], vectors_ref[2:3]
    back, sums_ref[0:1], sums_ref[1:2] = norm_grad(mixed_ref[...], gain, grad_ref[...])
    vit_grad = resid_ref[...] + back
    out_ref[...] = vit_grad
    low = (gate_tanh * vit_grad).astype(bf16)
    low_ref[...] = low
    gate_sum = jnp.sum(vit_grad * adapt_ref[...], axis=0, keepdims=True)
    sums_ref[2:3] = gate_sum * (1.0 - gate_tanh * gate_tanh)
    sums_ref[3:4] = jnp.sum(low.astype(f32), axis=0, keepdims=True)


def mix_grad(vectors, grad_norm1, mixed, grad_resid, adapt_flat):
    args = (vectors, grad_norm1, mixed, grad_resid, adapt_flat)
    return kernel_call(
        mix_grad_kernel,
        "mix_backward",
        blocks_of(args),
        [shape_of(f32, TOKENS, D), shape_of(bf16, TOKENS, D), shape_of(f32, 4, D)],
    )(*args)


def adapt_grad_kernel(
    keep_ref, before_ref, inner_ref, after_ref, b_ref, i_ref, a_ref, taps_ref, low_ref, sums_ref, frame, frame_in
):
    fill_frame(frame, keep_ref, before_ref, inner_ref, after_ref)
    fill_frame(frame_in, keep_ref, b_ref, i_ref, a_ref)
    tap_sums = [jnp.zeros((GRID, D), f32) for tap in range(9)]
    bias_sum = jnp.zeros((GRID, D), f32)
    rows = []
    for row in range(ROWS):
        grads = frame_row(frame, row + 1, 0)
        total = jnp.zeros((GRID, D), f32)
        for row_step in range(3):
            for col_step in range(3):
                tap = row_step * 3 + col_step
                total = total + taps_ref[tap : tap + 1] * frame_row(
                    frame, row + 2 - row_step, 1 - col_step
                )
                tap_sums[tap] += grads * frame_row(frame_in, row + row_step, col_step - 1)
        rows.append(total)
    low = jnp.concatenate(rows, axis=0).astype(bf16)
    low_ref[...] = low
    for tap in range(9):
        sums_ref[tap : tap + 1] = jnp.sum(tap_sums[tap], axis=0, keepdims=True)
    sums_ref[9:10] = jnp.sum(low.astype(f32), axis=0, keepdims=True)


def adapt_grad(keep, grad_rims, input_rims, taps):
    args = (*grad_rims, *input_rims, taps)
    return kernel_call(
        adapt_grad_kernel,
        "adapter_backward",
        [in_smem()] + blocks_of(args),
        [shape_of(bf16, TOKENS, D), shape_of(f32, 10, D)],
        [pltpu.VMEM((GRID_FRAME, D), f32), pltpu.VMEM((GRID_FRAME, D), f32)],
    )(keep, *args)


def gelu_parts(hidden):
    below = 0.5 * (1.0 + lax.erf(hidden * (0.5**0.5)))
    slope = below + hidden * jnp.exp(-0.5 * hidden * hidden) * 0.3989422804014327
    return hidden * below, slope


def mlp_kernel(
    norm_ref, cot_ref, fc1_ref, bias_ref, fc2_ref, out_in, grad_in, out_ref, grad_ref, g1_ref, gb_ref, g2_ref
):
    @pl.when(pl.program_id(0) == 0)
    def _():
        out_ref[...] = out_in[...]
        grad_ref[...] = grad_in[...]

    norm, cot, fc1, fc2 = norm_ref[...], cot_ref[...], fc1_ref[...], fc2_ref[...]
    hidden = jnp.dot(norm, fc1, preferred_element_type=f32) + bias_ref[...]
    act, slope = gelu_parts(hidden)
    act = act.astype(bf16)
    out_ref[...] += jnp.dot(act, fc2, preferred_element_type=f32)
    grad_hidden = (slope * dot_nt(cot, fc2)).astype(bf16)
    g2_ref[...] = dot_tn(act, cot).astype(bf16)
    g1_ref[...] = dot_tn(norm, grad_hidden).astype(bf16)
    gb_ref[...] = jnp.sum(grad_hidden.astype(f32), axis=0, keepdims=True)
    grad_ref[...] += dot_nt(grad_hidden, fc1)


def mlp_piece(norm, cotangent, fc1, bias, fc2, out_so_far, grad_so_far):
    hidden = fc1.shape[1]
    step = next(size for size in (512, 256, 128) if hidden % size == 0)
    columns = pl.BlockSpec((D, step), lambda i: (0, i))
    down = pl.BlockSpec((step, D), lambda i: (i, 0))
    bias_block = pl.BlockSpec((1, step), lambda i: (0, i))
    tokens = whole(TOKENS, D)
    return pl.pallas_call(
        mlp_kernel,
        grid=(hidden // step,),
        in_specs=[tokens, tokens, columns, bias_block, down, tokens, tokens],
        out_specs=[tokens, tokens, columns, bias_block, down],
        out_shape=[
            shape_of(f32, TOKENS, D),
            shape_of(f32, TOKENS, D),
            shape_of(bf16, D, hidden),
            shape_of(f32, 1, hidden),
            shape_of(bf16, hidden, D),
        ],
        compiler_params=pltpu.CompilerParams(vmem_limit_bytes=40 << 20),
        name="mlp_piece",
    )(norm, cotangent, fc1, bias[None], fc2, out_so_far, grad_so_far)


def pick_columns(weight, parts, groups):
    rows, wide = weight.shape
    width = wide // parts // groups

    def kernel(index_ref, weight_ref, out_ref):
        for index in range(groups):

            @pl.when(index_ref[0] == index)
            def _():
                for part in range(parts):
                    begin = (part * groups + index) * width
                    out_ref[:, part * width : (part + 1) * width] = weight_ref[
                        :, begin : begin + width
                    ]

    return kernel_call(
        kernel, "pick_columns", [in_smem(), whole(rows, wide)], [shape_of(bf16, rows, wide // groups)]
    )(lax.axis_index(GRP)[None], weight)[0]


def place_columns(pieces, parts):
    groups = len(pieces)
    rows, narrow = pieces[0].shape
    width = narrow // parts

    def kernel(index_ref, *refs):
        inputs, out_ref = refs[:groups], refs[groups]
        for index in range(groups):

            @pl.when(index_ref[0] == index)
            def _():
                for place in range(groups):
                    for part in range(parts):
                        begin = (part * groups + (place ^ index)) * width
                        out_ref[:, begin : begin + width] = inputs[place][
                            :, part * width : (part + 1) * width
                        ].astype(f32)

    return kernel_call(
        kernel, "place_columns", [in_smem()] + blocks_of(pieces), [shape_of(f32, rows, narrow * groups)]
    )(lax.axis_index(GRP)[None], *pieces)[0]


def bundle_rows(vectors, parts):
    vectors = [vector.reshape(1, -1) for vector in vectors]
    length = sum(vector.shape[1] for vector in vectors) // parts

    def kernel(*refs):
        inputs, out_ref = refs[:-1], refs[-1]
        begin = 0
        for ref in inputs:
            size = ref.shape[1] // parts
            for part in range(parts):
                out_ref[part : part + 1, begin : begin + size] = ref[
                    :, part * size : (part + 1) * size
                ]
            begin += size

    rows = kernel_call(kernel, "bundle_rows", blocks_of(vectors), [shape_of(f32, parts, length)])(
        *vectors
    )[0]
    return rows.reshape(-1, LANES)


def joint_grads(norm, grad_pieces, context, out_pieces):
    part, count = out_pieces[0].shape[1], len(out_pieces)

    def kernel(norm_ref, context_ref, *refs):
        for place in range(count):
            grads, outs, result = refs[place], refs[count + place], refs[2 * count + place]
            result[:, : 3 * part] = dot_tn(norm_ref[...], grads[...]).astype(bf16)
            result[:, 3 * part :] = dot_tn(context_ref[...], outs[...]).astype(bf16)

    return kernel_call(
        kernel,
        "joint_grads",
        blocks_of((norm, context, *grad_pieces, *out_pieces)),
        [shape_of(bf16, D, 4 * part)] * count,
    )(norm, context, *grad_pieces, *out_pieces)


def side_by_side(vectors):
    vectors = [vector.reshape(1, -1) for vector in vectors]

    def kernel(*refs):
        begin = 0
        for ref in refs[:-1]:
            size = ref.shape[1]
            refs[-1][:, begin : begin + size] = ref[...].astype(f32)
            begin += size

    length = sum(vector.shape[1] for vector in vectors)
    joined = kernel_call(kernel, "side_by_side", blocks_of(vectors), [shape_of(f32, 1, length)])(
        *vectors
    )[0]
    return joined.reshape(-1, LANES)


def band_slices(cells, size_class):
    bands = []
    for image, image_cells in enumerate(cells):
        step = size_class[image] // BANDS * SIDE
        for band in range(BANDS):
            bands.append(lax.dynamic_slice_in_dim(image_cells, band * step, BAND_CELLS, 0))
    return jnp.stack(bands)


def pool_tables(size_class, mask_bands):
    sizes = jnp.repeat(size_class, BANDS)[:, None, None]
    out_ids = lax.broadcasted_iota(jnp.int32, (1, TOKENS, 1), 1)
    out_row, out_col = out_ids // GRID, out_ids % GRID
    cell_ids = lax.broadcasted_iota(jnp.int32, (1, 1, BAND_CELLS), 2)
    cell_row, cell_col = cell_ids // SIDE, cell_ids % SIDE
    row_hit = (out_row * sizes // GRID <= cell_row) & (
        cell_row < ((out_row + 1) * sizes + GRID - 1) // GRID
    )
    col_hit = (out_col * sizes // GRID <= cell_col) & (
        cell_col < ((out_col + 1) * sizes + GRID - 1) // GRID
    )
    return jnp.where(row_hit & col_hit, mask_bands[:, None, :], 0).astype(bf16)


def batched(left, right, left_dim, right_dim):
    return lax.dot_general(
        left, right, (((left_dim,), (right_dim,)), ((0,), (0,))), preferred_element_type=f32
    )


class Small(NamedTuple):
    ln1_gain: Any
    ln1_bias: Any
    qv_bias: Any
    out_bias: Any
    ln2_gain: Any
    ln2_bias: Any
    fc1_bias: Any
    fc2_bias: Any
    conv_gain: Any
    conv_bias: Any
    pw1_bias: Any
    pw2_bias: Any
    layer_scale: Any
    proj_bias: Any
    dw3_weight: Any
    dw3_bias: Any
    gate: Any


def body(
    vit_in,
    hires,
    size_class,
    pool_mask,
    cotangent,
    ln1_gain,
    ln1_bias,
    qkv_weight,
    qv_bias,
    out_weight,
    out_bias,
    ln2_gain,
    ln2_bias,
    fc1_weight,
    fc1_bias,
    fc2_weight,
    fc2_bias,
    dw7_weight,
    dw7_bias,
    conv_gain,
    conv_bias,
    pw1_weight,
    pw1_bias,
    pw2_weight,
    pw2_bias,
    layer_scale,
    proj_weight,
    proj_bias,
    dw3_weight,
    dw3_bias,
    gate,
):
    parts = lax.axis_size(CHAN)
    groups = lax.axis_size(GRP)
    chan_index = lax.axis_index(CHAN)
    band_index = chan_index % BANDS
    grp_index = lax.axis_index(GRP)
    width = hires.shape[1] * parts
    places = list(range(groups))
    part = D // groups

    along_chan = [(CHAN, bit) for bit in reversed(range(count_bits(CHAN)))]
    along_grp = [(GRP, bit) for bit in reversed(range(count_bits(GRP)))]
    conv_plan = along_chan + [step for step in along_grp if step[1] != PAIR]
    vit_plan = along_chan + along_grp

    rows = qkv_weight.shape[0]
    qkv_out_own = jnp.concatenate(
        [
            my_part(qkv_weight.reshape(rows, 3, groups, -1), 2).reshape(rows, -1),
            my_part(out_weight.reshape(rows, groups, -1), 1),
        ],
        axis=1,
    )
    qkv_out_flow = Flow(gather_crosswise(qkv_out_own, vit_plan))
    proj_flow = Flow(
        gather_crosswise(my_part(proj_weight.reshape(-1, groups, part), 1), vit_plan)
    )
    smalls = Small(
        ln1_gain,
        ln1_bias,
        qv_bias,
        out_bias,
        ln2_gain,
        ln2_bias,
        fc1_bias,
        fc2_bias,
        conv_gain,
        conv_bias,
        pw1_bias,
        pw2_bias,
        layer_scale,
        proj_bias,
        dw3_weight.reshape(-1),
        dw3_bias,
        gate,
    )
    small_flow = Flow(gather(side_by_side(smalls), along_chan))
    pw1_flow = Flow(gather(pick_columns(pw1_weight, parts, groups), conv_plan))
    flows = []

    def half_way(value):
        value = sync(value, small_flow)
        value, pw2_part = sync(
            (value, pw2_weight), small_flow, qkv_out_flow, proj_flow, pw1_flow
        )
        flows.append(Flow(gather(my_part(pw2_part.reshape(groups, -1, width), 0), conv_plan)))
        return value

    conv_bands, masked_bands, conv_saved = conv_forward(
        hires, size_class, dw7_weight, dw7_bias, half_way
    )
    pw2_flow = flows[0]
    conv_bands, masked_bands = sync(
        (conv_bands, masked_bands), qkv_out_flow, proj_flow
    )
    conv_recv = all_to_all(conv_bands)
    masked_bands, fc1_late, fc2_late = lax.optimization_barrier(
        (masked_bands, fc1_weight, fc2_weight)
    )
    fc1_own = my_part(fc1_late.reshape(rows, parts, groups, -1), 2).reshape(rows, -1)
    fc2_own = my_part(fc2_late.reshape(groups, -1, D), 0)
    tables = pool_tables(size_class, band_slices(pool_mask, size_class))
    all_counts = jnp.maximum(jnp.sum(tables.astype(f32), axis=2), 1.0)
    pooled_in = (batched(tables, masked_bands, 2, 1) / all_counts[:, :, None]).astype(bf16)
    table = lax.dynamic_index_in_dim(tables, chan_index, 0, keepdims=False)
    table_pair = jnp.stack([table, flip(table, GRP, PAIR)])
    count_raw = jnp.sum(table.astype(f32), axis=1)
    pool_count = jnp.maximum(count_raw, 1.0)[:, None]
    count_part = count_raw[:, None] / pool_count
    pooled_in = sync(pooled_in, pw1_flow, pw2_flow, qkv_out_flow, proj_flow, small_flow)
    small_full = small_flow.finish()[0].reshape(parts, -1)
    full, begin = [], 0
    for value in smalls:
        full.append(small_full[:, begin : begin + value.shape[0]].reshape(-1))
        begin += value.shape[0]
    small = Small(*full)
    dw3_taps = small.dw3_weight.reshape(parts, 9, -1).transpose(1, 0, 2).reshape(9, D)

    def hidden_bias(all_units, place):
        split = all_units.reshape(parts, groups, -1)
        return lax.dynamic_index_in_dim(split, grp_index ^ place, 1, keepdims=False).reshape(-1)

    normed_own = conv_norm_forward(conv_recv, small.conv_gain, small.conv_bias)
    normed_other = flip(normed_own, GRP, PAIR)
    normed_own = sync(normed_own, pw1_flow, qkv_out_flow, proj_flow)
    normed_own = sync(normed_own, pw2_flow)
    fc1_flow = Flow(gather_crosswise(fc1_own, vit_plan))
    fc2_flow = Flow(gather_crosswise(fc2_own, vit_plan))
    normed_other = sync(normed_other, fc1_flow, fc2_flow)
    normed_low = jnp.concatenate([normed_own, normed_other], axis=0)
    pw1 = pw1_flow.finish()
    conv_places = sorted(pw1)
    conv_act, conv_slope, branch = {}, {}, None
    for place in conv_places:
        hidden = matmul(normed_low, pw1[place]) + hidden_bias(small.pw1_bias, place)
        conv_act[place], conv_slope[place] = gelu_and_slope(hidden)
    conv_act, pooled_in = sync((conv_act, pooled_in), pw2_flow, fc1_flow, fc2_flow)
    pw2 = pw2_flow.finish()
    pooled_in = all_to_all(pooled_in)
    branch = matmul(conv_act[conv_places[0]], pw2[conv_places[0]])
    branch, pooled_in = sync((branch, pooled_in), fc1_flow, fc2_flow)
    for place in conv_places[1:]:
        branch = branch + matmul(conv_act[place], pw2[place])
    pooled_part = batched(
        table_pair, branch.astype(bf16).reshape(2, BAND_CELLS, width), 2, 1
    )
    pooled_other = flip(pooled_part[1].astype(bf16), GRP, PAIR)
    pooled_sum = pooled_part[0] + pooled_other.astype(f32)
    pooled_branch = pooled_sum / pool_count + small.pw2_bias * count_part
    pooled_in = pooled_in.transpose(1, 0, 2).reshape(TOKENS, width).astype(f32)
    pooled_low = (pooled_in + small.layer_scale * pooled_branch).astype(bf16)

    def in_columns(pieces):
        return jnp.concatenate(reorder([pieces[place] for place in places]), axis=1)

    def column_parts(value):
        return reorder(jnp.split(value, groups, axis=1))

    proj = proj_flow.finish()
    qkv_out = qkv_out_flow.finish()
    adapt = in_columns({place: matmul(pooled_low, proj[place]) for place in places})
    adapt_low = (adapt + small.proj_bias).astype(bf16)
    adapt_rims = (
        shifted(adapt_low[TOKENS - GRID :], CHAN, 1),
        adapt_low,
        shifted(adapt_low[:GRID], CHAN, -1),
    )
    keep = jnp.stack([band_index > 0, band_index < BANDS - 1]).astype(jnp.int32)
    gate_tanh = jnp.tanh(small.gate)
    vectors = jnp.stack([small.dw3_bias, gate_tanh, small.ln1_gain, small.ln1_bias])
    adapt_flat, mixed, norm1_low = mix_forward(keep, *adapt_rims, dw3_taps, vectors, vit_in)
    qv_split = small.qv_bias.reshape(2, groups, part)
    qkv_parts = []
    for place in places:
        biases = lax.dynamic_index_in_dim(qv_split, grp_index ^ place, 1, keepdims=False)
        bias = jnp.concatenate([biases[0], jnp.zeros((part,), f32), biases[1]])
        qkv_parts.append((matmul(norm1_low, qkv_out[place][:, : 3 * part]) + bias).astype(bf16))
    share = D // BANDS

    def band_shares(pieces):
        ratio = max(1, groups // BANDS)
        kinds = pieces[0].shape[1] // part
        if groups <= BANDS:
            cuts = []
            for piece in pieces:
                split = piece.reshape(TOKENS, kinds, BANDS // groups, share)
                cuts += [split[:, :, i].reshape(TOKENS, -1) for i in range(BANDS // groups)]
            return cuts
        joined = []
        for band in range(BANDS):
            own = [p.reshape(TOKENS, kinds, part) for p in pieces[band * ratio : (band + 1) * ratio]]
            joined.append(jnp.concatenate(own, axis=2).reshape(TOKENS, -1))
        return joined

    def grp_parts(shares):
        ratio = max(1, groups // BANDS)
        kinds = shares[0].shape[1] // share
        split = [s.reshape(TOKENS, kinds, share) for s in shares]
        if groups <= BANDS:
            each = BANDS // groups
            return [
                jnp.concatenate(split[i * each : (i + 1) * each], axis=2).reshape(TOKENS, -1)
                for i in range(groups)
            ]
        return [
            split[i // ratio][:, :, i % ratio * part : (i % ratio + 1) * part].reshape(TOKENS, -1)
            for i in range(groups)
        ]

    received = sync(band_exchange(band_shares(qkv_parts)), fc1_flow, fc2_flow)
    context, qkv_heads = attention(received)
    context_back = band_return(list(context))
    context_low = jnp.concatenate(reorder(grp_parts(context_back)), axis=1)
    attn = in_columns(
        {place: matmul(context_low, qkv_out[place][:, 3 * part :]) for place in places}
    )
    resid = mixed + attn + small.out_bias
    norm2, ln2_pullback = jax.vjp(norm_vit, resid, small.ln2_gain, small.ln2_bias)
    norm2_low = norm2.astype(bf16)
    vit_out = resid + small.fc2_bias
    grad_norm2 = jnp.zeros((TOKENS, D), f32)
    fc1, fc2 = fc1_flow.finish(), fc2_flow.finish()
    fc1_grads, fc2_grads, fc1_bias_grads = {}, {}, []
    for place in places:
        vit_out, grad_norm2, fc1_grads[place], bias_grad, fc2_grads[place] = mlp_piece(
            norm2_low,
            cotangent,
            fc1[place],
            hidden_bias(small.fc1_bias, place),
            fc2[place],
            vit_out,
            grad_norm2,
        )
        fc1_bias_grads.append(bias_grad.reshape(parts, -1))

    fc2_sum = Flow(scatter_and_spread(fc2_grads, vit_plan, crosswise_sum))
    fc1_sum = Flow(scatter_and_spread(fc1_grads, vit_plan, crosswise_sum))
    grads = SimpleNamespace(fc2_bias=column_sum(cotangent))

    def hidden_bias_grad(parts_rel):
        return jnp.stack(reorder(parts_rel), axis=1).reshape(-1)

    grads.fc1_bias = hidden_bias_grad(fc1_bias_grads)
    grad_resid_part, grads.ln2_gain, grads.ln2_bias = ln2_pullback(grad_norm2)
    grad_resid = cotangent.astype(f32) + grad_resid_part
    grad_attn_low = grad_resid.astype(bf16)
    grads.out_bias = column_sum(grad_attn_low)
    grad_attn_rel = column_parts(grad_attn_low)
    grad_context = sum(
        right_grad(grad_attn_rel[place], qkv_out[place][:, 3 * part :]) for place in places
    )
    context_grad_rel = band_shares(column_parts(grad_context.astype(bf16)))
    context_grads = sync(band_exchange(context_grad_rel), fc2_sum)
    qkv_grad_heads = attention_grad(qkv_heads, context_grads)
    qkv_grad_parts = grp_parts(band_return(list(qkv_grad_heads)))
    bias_rel = reorder([column_sum(g) for g in qkv_grad_parts])
    grads.qv_bias = jnp.concatenate(
        [g[:part] for g in bias_rel] + [g[2 * part :] for g in bias_rel]
    )
    grad_norm1 = sum(
        right_grad(qkv_grad_parts[place], qkv_out[place][:, : 3 * part]) for place in places
    )
    vit_grad, grad_conv3_low, mix_sums = mix_grad(vectors, grad_norm1, mixed, grad_resid, adapt_flat)
    grads.ln1_gain, grads.ln1_bias, grads.gate, grads.dw3_bias = mix_sums
    grad_rims = (
        shifted(grad_conv3_low[TOKENS - GRID :], CHAN, 1),
        grad_conv3_low,
        shifted(grad_conv3_low[:GRID], CHAN, -1),
    )
    grad_rims = sync(grad_rims, fc1_sum)
    joint = joint_grads(norm1_low, qkv_grad_parts, context_low, grad_attn_rel)
    joint_sum = Flow(
        scatter_and_spread(dict(enumerate(joint)), vit_plan, crosswise_sum)
    )
    grad_adapt_low, adapt_sums = adapt_grad(keep, grad_rims, adapt_rims, dw3_taps)
    grads.dw3_weight = adapt_sums[:9].reshape(9, parts, -1).transpose(1, 0, 2).reshape(-1)
    grads.proj_bias = adapt_sums[9]
    grad_adapt_rel = column_parts(grad_adapt_low)
    grad_pooled = sum(right_grad(grad_adapt_rel[place], proj[place]) for place in places)
    grad_pooled = grad_pooled.astype(bf16).astype(f32)
    grad_pool_sum = grad_pooled / pool_count
    scaled_own = (small.layer_scale * grad_pool_sum).astype(bf16)
    scaled_other = flip(scaled_own, GRP, PAIR)
    grads.layer_scale = jnp.sum(grad_pooled * pooled_branch, axis=0)
    grads.pw2_bias = small.layer_scale * jnp.sum(grad_pooled * count_part, axis=0)
    proj_sum = Flow(
        scatter_and_spread(
            {place: left_grad(pooled_low, grad_adapt_rel[place]) for place in places},
            vit_plan,
            crosswise_sum,
        )
    )
    scaled_other = sync(scaled_other, fc2_sum)
    grad_branch_low = (
        batched(table_pair, jnp.stack([scaled_own, scaled_other]), 1, 1)
        .astype(bf16)
        .reshape(2 * BAND_CELLS, width)
    )
    resid_back = all_to_all(
        grad_pool_sum.astype(bf16).reshape(TOKENS, parts, -1).transpose(1, 0, 2)
    )
    pw2_grads = {
        place: left_grad(conv_act[place], grad_branch_low) for place in reversed(conv_places)
    }
    grad_branch_low, pw2_grads = sync(
        (grad_branch_low, pw2_grads), fc1_sum, joint_sum, proj_sum
    )
    pw2_sum = Flow(scatter_and_spread(pw2_grads, conv_plan))
    grad_hidden, grad_normed_pair = {}, None
    for place in reversed(conv_places):
        grad_act = right_grad(grad_branch_low, pw2[place])
        grad_hidden[place] = (conv_slope[place].astype(f32) * grad_act).astype(bf16)
        if place == conv_places[-1]:
            grad_branch_low, grad_hidden = sync(
                (grad_branch_low, grad_hidden), pw2_sum, fc2_sum
            )
    for place in reversed(conv_places):
        product = right_grad(grad_hidden[place], pw1[place])
        grad_normed_pair = product if grad_normed_pair is None else grad_normed_pair + product
    grad_normed_pair, grad_hidden = sync(
        (grad_normed_pair, grad_hidden), joint_sum, fc1_sum, fc2_sum
    )
    grad_normed_other = flip(grad_normed_pair[BAND_CELLS:].astype(bf16), GRP, PAIR)
    pw1_grads = {}
    pw1_bias_grads = [jnp.zeros((parts, pw1_weight.shape[1] // parts // groups), f32)] * groups
    for place in reversed(conv_places):
        pw1_grads[place] = left_grad(normed_low, grad_hidden[place])
        pw1_bias_grads[place] = column_sum(grad_hidden[place]).reshape(parts, -1)
    pw1_sum = Flow(scatter_and_spread(pw1_grads, conv_plan))
    grads.pw1_bias = hidden_bias_grad(pw1_bias_grads)
    grad_normed_other, resid_back = sync(
        (grad_normed_other, resid_back), pw1_sum, pw2_sum, fc2_sum, fc1_sum, proj_sum
    )
    grad_conv_bands, norm_sums = conv_norm_backward(
        conv_recv, small.conv_gain, grad_normed_pair[:BAND_CELLS], grad_normed_other
    )
    grads.conv_gain, grads.conv_bias = norm_sums
    grad_conv_back = all_to_all(grad_conv_bands)
    resid_bands = batched(tables, resid_back, 1, 1).astype(bf16)
    others = (pw1_sum, pw2_sum, joint_sum, proj_sum, fc2_sum, fc1_sum)
    grad_conv_back = sync(grad_conv_back, *others)

    def half_way_back(value):
        value, bundle = lax.optimization_barrier(
            (sync(value, *others), bundle_rows(Small(**vars(grads)), parts))
        )
        flows.append(Flow(total_sum(bundle, vit_plan)))
        return value

    hires_grad, dw7_grads = conv_backward(conv_saved, grad_conv_back, resid_bands, half_way_back)
    bundle_sum = flows[1]
    hires_grad, dw7_grads = sync((hires_grad, dw7_grads), bundle_sum, *others)
    for axis, bit in along_grp:
        dw7_grads = dw7_grads + flip(dw7_grads, axis, bit)
    total = bundle_sum.finish().reshape(-1)
    sums, begin = [], 0
    for value in smalls:
        sums.append(total[begin : begin + value.shape[0]])
        begin += value.shape[0]
    sums = Small(*sums)

    grad_fc1 = place_columns(fc1_sum.finish(), parts)
    grad_fc2 = jnp.concatenate(reorder(fc2_sum.finish()), axis=0)
    grad_proj = jnp.concatenate(reorder(proj_sum.finish()), axis=1)
    joint_all = reorder(joint_sum.finish())
    grad_qkv = jnp.concatenate(
        [piece[:, kind * part : (kind + 1) * part] for kind in range(3) for piece in joint_all],
        axis=1,
    )
    grad_out = jnp.concatenate([piece[:, 3 * part :] for piece in joint_all], axis=1)
    grad_pw2 = jnp.concatenate(reorder(pw2_sum.finish()), axis=0)
    grad_pw1 = place_columns(pw1_sum.finish(), parts)
    return (
        vit_out,
        vit_grad,
        hires_grad,
        sums.ln1_gain,
        sums.ln1_bias,
        grad_qkv.astype(f32),
        sums.qv_bias,
        grad_out.astype(f32),
        sums.out_bias,
        sums.ln2_gain,
        sums.ln2_bias,
        grad_fc1,
        sums.fc1_bias,
        grad_fc2.astype(f32),
        sums.fc2_bias,
        dw7_grads[: KERNEL * KERNEL],
        dw7_grads[KERNEL * KERNEL],
        sums.conv_gain,
        sums.conv_bias,
        grad_pw1,
        sums.pw1_bias,
        grad_pw2.astype(f32),
        sums.pw2_bias,
        sums.layer_scale,
        grad_proj.astype(f32),
        sums.proj_bias,
        sums.dw3_weight.reshape(9, -1),
        sums.dw3_bias,
        sums.gate,
    )


def solution(mesh):
    in_specs = (
        P((GRP, CHAN), None),
        P(GRP, CHAN, None),
        P(GRP),
        P(GRP, None),
        P((GRP, CHAN), None),
        P(CHAN),
        P(CHAN),
        P(CHAN, None),
        P(CHAN),
        P(CHAN, None),
        P(CHAN),
        P(CHAN),
        P(CHAN),
        P(CHAN, None),
        P(CHAN),
        P(CHAN, None),
        P(CHAN),
        P(None, CHAN),
        P(CHAN),
        P(CHAN),
        P(CHAN),
        P(CHAN, None),
        P(CHAN),
        P(CHAN, None),
        P(CHAN),
        P(CHAN),
        P(CHAN, None),
        P(CHAN),
        P(None, CHAN),
        P(CHAN),
        P(CHAN),
    )
    out_specs = (
        P((GRP, CHAN), None),
        P((GRP, CHAN), None),
        P(GRP, CHAN, None),
        P(CHAN),
        P(CHAN),
        P(CHAN, None),
        P(CHAN),
        P(CHAN, None),
        P(CHAN),
        P(CHAN),
        P(CHAN),
        P(CHAN, None),
        P(CHAN),
        P(CHAN, None),
        P(CHAN),
        P(None, CHAN),
        P(CHAN),
        P(CHAN),
        P(CHAN),
        P(CHAN, None),
        P(CHAN),
        P(CHAN, None),
        P(CHAN),
        P(CHAN),
        P(CHAN, None),
        P(CHAN),
        P(None, CHAN),
        P(CHAN),
        P(CHAN),
    )
    return jax.shard_map(body, mesh=mesh, in_specs=in_specs, out_specs=out_specs, check_vma=False)
```

```python
from functools import partial
from types import SimpleNamespace
from typing import Any, NamedTuple

import jax
import jax.numpy as jnp
from jax import lax
from jax.experimental import pallas as pl
from jax.experimental.pallas import tpu as pltpu
from jax.sharding import PartitionSpec as P

D = 1024
HEADS = 16
HEAD_DIM = 64
KERNEL = 7
GRID = 24
BANDS = 4
SIDE = 2 * GRID
CELLS = SIDE * SIDE
BAND_CELLS = CELLS // BANDS
ROWS = GRID // BANDS
TOKENS = ROWS * GRID
PAIR = 1

EPS_VIT = 1e-05
EPS_CONV = 1e-06

CHAN = "chan"
GRP = "grp"

f32 = jnp.float32
bf16 = jnp.bfloat16


def flip(value, axis, bit):
    return lax.ppermute(value, axis, [(i, i ^ (1 << bit)) for i in range(lax.axis_size(axis))])


def bit_at(axis, bit):
    return (lax.axis_index(axis) >> bit) & 1


def shifted(value, axis, steps):
    count = lax.axis_size(axis)
    first, last = (max(0, -steps), min(count, count - steps))
    return lax.ppermute(value, axis, [(source, source + steps) for source in range(first, last)])


def count_bits(axis):
    return lax.axis_size(axis).bit_length() - 1


def reorder(pieces, axis=GRP):
    for bit in range(count_bits(axis)):
        swap = bit_at(axis, bit) == 1
        pieces = [
            jnp.where(swap, pieces[place ^ (1 << bit)], pieces[place])
            for place in range(len(pieces))
        ]
    return pieces


def chan_merge(own, got, bit):
    upper = bit_at(CHAN, bit) == 1
    both = jnp.stack([jnp.where(upper, got, own), jnp.where(upper, own, got)], axis=1)
    return both.reshape((2 * own.shape[0],) + own.shape[1:])


def gather(block, plan):
    pieces = {0: block[None]}
    for axis, bit in plan:
        got = yield {place: flip(piece, axis, bit) for place, piece in pieces.items()}
        if axis == CHAN:
            pieces = {place: chan_merge(pieces[place], got[place], bit) for place in pieces}
        else:
            pieces.update({place ^ (1 << bit): piece for place, piece in got.items()})
    return {
        place: piece.reshape((-1,) + piece.shape[2:]) for place, piece in sorted(pieces.items())
    }


def flip_crosswise(value, swapped):
    groups, parts = lax.axis_size(GRP), lax.axis_size(CHAN)
    pairs = []
    for member in range(groups):
        for place in range(parts):
            other = (member, place ^ 1) if member % 2 == swapped else (member ^ 1 << PAIR, place)
            pairs.append((member * parts + place, other[0] * parts + other[1]))
    return lax.ppermute(value, (GRP, CHAN), pairs)


def gather_crosswise(block, plan):
    own = block[None]
    for axis, bit in plan:
        if axis == CHAN and bit > 0:
            got = yield flip(own, axis, bit)
            own = chan_merge(own, got, bit)
    first = yield flip_crosswise(own, 0)
    second = yield (flip_crosswise(own, 1), flip_crosswise(first, 1))
    even = lax.axis_index(GRP) % 2 == 0
    beside = jnp.where(even, first, second[0])
    across = jnp.where(even, second[0], first)
    pieces = {0: chan_merge(own, beside, 0), 1 << PAIR: chan_merge(across, second[1], 0)}
    for axis, bit in plan:
        if axis == GRP and bit != PAIR:
            got = yield {place: flip(piece, axis, bit) for place, piece in pieces.items()}
            pieces.update({place ^ (1 << bit): piece for place, piece in got.items()})
    return {
        place: piece.reshape((-1,) + piece.shape[2:]) for place, piece in sorted(pieces.items())
    }


class Flow:
    def __init__(self, steps):
        self.steps = steps
        self.pending = next(steps)
        self.result = None

    def advance(self, got):
        try:
            self.pending = self.steps.send(got)
        except StopIteration as stop:
            self.pending, self.result = None, stop.value

    def finish(self):
        while self.pending is not None:
            self.advance(self.pending)
        return self.result


def sync(value, *flows):
    flows = [flow for flow in flows if flow.pending is not None]
    value, arrived = lax.optimization_barrier((value, [flow.pending for flow in flows]))
    for flow, got in zip(flows, arrived):
        flow.advance(got)
    return value


def added(left, right):
    return (left.astype(f32) + right.astype(f32)).astype(left.dtype)


def scatter_sum(pieces, plan):
    parts = lax.axis_size(CHAN)
    pieces = {
        place: piece.reshape((parts, piece.shape[0] // parts) + piece.shape[1:])
        for place, piece in pieces.items()
    }
    for axis, bit in reversed(plan):
        if axis == CHAN:
            mine = bit_at(CHAN, bit)
            kept, sent = {}, {}
            for place, piece in pieces.items():
                halves = piece.reshape((piece.shape[0] // 2, 2) + piece.shape[1:])
                kept[place] = lax.dynamic_index_in_dim(halves, mine, 1, keepdims=False)
                sent[place] = lax.dynamic_index_in_dim(halves, 1 - mine, 1, keepdims=False)
        else:
            kept = {place: piece for place, piece in pieces.items() if not place >> bit & 1}
            sent = {place: pieces[place ^ (1 << bit)] for place in kept}
        got = yield {place: flip(piece, axis, bit) for place, piece in sent.items()}
        pieces = {place: added(kept[place], got[place]) for place in kept}
    return pieces[0][0]


def halve(piece, bit):
    mine = bit_at(CHAN, bit)
    halves = piece.reshape((piece.shape[0] // 2, 2) + piece.shape[1:])
    return [lax.dynamic_index_in_dim(halves, i, 1, keepdims=False) for i in (mine, 1 - mine)]


def crosswise_sum(pieces, plan):
    parts = lax.axis_size(CHAN)
    pieces = {
        place: piece.reshape((parts, piece.shape[0] // parts) + piece.shape[1:])
        for place, piece in pieces.items()
    }
    for axis, bit in reversed(plan):
        if axis == GRP and bit != PAIR:
            kept = {place: piece for place, piece in pieces.items() if not place >> bit & 1}
            sent = {place: pieces[place ^ (1 << bit)] for place in kept}
            got = yield {place: flip(piece, axis, bit) for place, piece in sent.items()}
            pieces = {place: added(kept[place], got[place]) for place in kept}
    even = lax.axis_index(GRP) % 2 == 0
    own, beside = halve(pieces[0], 0)
    across, far = halve(pieces[1 << PAIR], 0)
    got = yield (
        flip_crosswise(jnp.where(even, across, beside), 1),
        flip_crosswise(far, 1),
    )
    own = added(own, got[0])
    other = added(jnp.where(even, beside, across), got[1])
    got = yield flip_crosswise(other, 0)
    own = added(own, got)
    for axis, bit in reversed(plan):
        if axis == CHAN and bit > 0:
            kept, sent = halve(own, bit)
            got = yield flip(sent, axis, bit)
            own = added(kept, got)
    return own[0]


def scatter_and_spread(pieces, plan, sums=scatter_sum):
    block = yield from sums(pieces, plan)
    pieces = {0: lax.optimization_barrier(block)}
    for bit in reversed(range(count_bits(GRP))):
        got = yield {place: flip(piece, GRP, bit) for place, piece in pieces.items()}
        pieces.update({place ^ (1 << bit): piece for place, piece in got.items()})
    return [pieces[place] for place in range(len(pieces))]


def total_sum(bundle, plan):
    total = yield from scatter_sum({0: bundle}, [step for step in plan if step[0] == CHAN])
    for axis, bit in plan:
        if axis == GRP:
            got = yield flip(total, axis, bit)
            total = total + got
    return total


def my_part(value, dim):
    return lax.dynamic_index_in_dim(value, lax.axis_index(GRP), dim, keepdims=False)


def pick(pieces, index):
    for bit in range(len(pieces).bit_length() - 1):
        odd = (index >> bit) & 1 == 1
        pieces = [
            jnp.where(odd, pieces[2 * i + 1], pieces[2 * i]) for i in range(len(pieces) // 2)
        ]
    return pieces[0]


def band_exchange(pieces):
    band = lax.axis_index(CHAN) % BANDS
    count = lax.axis_size(CHAN)
    received = [pick(pieces, band)]
    for apart in range(1, BANDS):
        sent = pick(pieces, band ^ apart)
        received.append(lax.ppermute(sent, CHAN, [(i, i ^ apart) for i in range(count)]))
    return received


def band_return(received):
    band = lax.axis_index(CHAN) % BANDS
    count = lax.axis_size(CHAN)
    back = [received[0]]
    for apart in range(1, BANDS):
        back.append(lax.ppermute(received[apart], CHAN, [(i, i ^ apart) for i in range(count)]))
    return [pick(back, place ^ band) for place in range(BANDS)]


def all_to_all(value):
    return lax.all_to_all(value, CHAN, split_axis=0, concat_axis=0, tiled=True)


def layer_norm(inputs, gain, shift_term, epsilon):
    mean_row = jnp.mean(inputs, axis=-1, keepdims=True)
    centred = inputs - mean_row
    variance = jnp.mean(centred * centred, axis=-1, keepdims=True)
    return centred * lax.rsqrt(variance + epsilon) * gain + shift_term


def norm_vit(inputs, gain, shift_term):
    return layer_norm(inputs, gain, shift_term, EPS_VIT)


def gelu_and_slope(inputs):
    below = 0.5 * (1.0 + lax.erf(inputs * (0.5**0.5)))
    slope = below + inputs * jnp.exp(-0.5 * inputs * inputs) * 0.3989422804014327
    return (inputs * below).astype(bf16), slope.astype(bf16)


def matmul(left, right):
    return jnp.dot(left, right, preferred_element_type=f32)


def left_grad(inputs, grads):
    return lax.dot_general(
        inputs, grads, (((0,), (0,)), ((), ())), preferred_element_type=f32
    ).astype(bf16)


def right_grad(grads, weight):
    return lax.dot_general(grads, weight, (((1,), (1,)), ((), ())), preferred_element_type=f32)


def column_sum(grads):
    return jnp.sum(grads.astype(f32), axis=0)


PITCH = SIDE + 8
HALF = KERNEL // 2
FRAME = (SIDE + 2 * HALF) * PITCH + 8
LANES = 128


def frame_at(row, col):
    return pl.multiple_of((row + HALF) * PITCH, 8) + 8 + col


def valid_row(row, sizes):
    cols = lax.broadcasted_iota(jnp.int32, (SIDE, LANES), 0)
    return jnp.where(row < sizes, cols, SIDE) < sizes


def whole(*shape):
    return pl.BlockSpec(shape, lambda *grid: (0,) * len(shape))


def in_smem():
    return pl.BlockSpec(memory_space=pltpu.SMEM)


def band_rows(step, band):
    return pl.ds(pl.multiple_of(step * band, 16), BAND_CELLS)


def convolve_tiles(sizes_ref, taps_ref, bias_ref, maps_ref, cells_ref, masked_ref, turned, framed, first=0):
    framed[...] = jnp.zeros_like(framed)
    for lane in range(0, maps_ref.shape[0], LANES):
        here = slice(first + lane, first + lane + LANES)
        for begin in range(0, CELLS, LANES):
            columns = maps_ref[lane : lane + LANES, begin : begin + LANES]
            turned[begin : begin + LANES] = columns.astype(f32).T
        sizes = sizes_ref[:, here]

        def fill(row, carry):
            cells = pl.ds(pl.multiple_of(row * SIDE, 16), SIDE)
            inner = jnp.where(valid_row(row, sizes), turned[cells], 0.0)
            framed[pl.ds(frame_at(row, 0), SIDE)] = inner
            masked_ref[cells, here] = inner.astype(bf16)
            return carry

        lax.fori_loop(0, SIDE, fill, 0)

        def convolve(row, carry):
            total = jnp.zeros((SIDE, LANES), f32) + bias_ref[:, here]
            for row_step in range(KERNEL):
                for col_step in range(KERNEL):
                    tap = row_step * KERNEL + col_step
                    total = total + taps_ref[tap : tap + 1, here] * framed[
                        pl.ds(frame_at(row + row_step - HALF, col_step - HALF), SIDE)
                    ]
            cells = pl.ds(pl.multiple_of(row * SIDE, 16), SIDE)
            cells_ref[cells, here] = jnp.where(valid_row(row, sizes), total, 0.0).astype(bf16)
            return carry

        lax.fori_loop(0, SIDE, convolve, 0)


def conv_forward_kernel(sizes_ref, taps_ref, bias_ref, maps_ref, cells_ref, masked_ref, turned, framed):
    convolve_tiles(sizes_ref, taps_ref, bias_ref, maps_ref, cells_ref, masked_ref, turned, framed)


def conv_forward_last_kernel(
    step_ref,
    sizes_ref,
    taps_ref,
    bias_ref,
    maps_ref,
    early_cells_ref,
    early_masked_ref,
    conv_ref,
    bands_ref,
    masked_ref,
    turned,
    framed,
    cells_ref,
):
    early, channels = early_cells_ref.shape[1], conv_ref.shape[2]
    cells_ref[:, :early] = early_cells_ref[...]
    masked_ref[:, :early] = early_masked_ref[...]
    convolve_tiles(
        sizes_ref, taps_ref, bias_ref, maps_ref, cells_ref, masked_ref, turned, framed, early
    )
    for image in range(masked_ref.shape[1] // channels):
        here = slice(image * channels, (image + 1) * channels)
        for band in range(BANDS):
            rows = band_rows(step_ref[image], band)
            conv_ref[image * BANDS + band] = cells_ref[rows, here]
            bands_ref[image * BANDS + band] = masked_ref[rows, here]


def conv_backward_kernel(
    step_ref,
    sizes_ref,
    taps_ref,
    masked_ref,
    grad_ref,
    resid_ref,
    *refs,
    first,
):
    (
        out_ref,
        tap_grad_ref,
        framed,
        framed_grad,
        field,
        sums,
        grad_cells,
        resid_cells,
    ) = refs[-8:]
    lanes, channels = masked_ref.shape[1], grad_ref.shape[2]
    framed[...] = jnp.zeros_like(framed)
    framed_grad[...] = jnp.zeros_like(framed_grad)
    grad_cells[...] = jnp.zeros_like(grad_cells)
    resid_cells[...] = jnp.zeros_like(resid_cells)
    for image in range(lanes // channels):
        here = slice(image * channels, (image + 1) * channels)
        for band in range(BANDS):
            rows = band_rows(step_ref[image], band)
            grad_cells[rows, here] = grad_ref[image * BANDS + band]
            resid_cells[rows, here] = resid_ref[image * BANDS + band]

    def in_eights(value):
        return jnp.sum(value.reshape(SIDE // 8, 8, LANES), axis=0)

    for tile in range(0, out_ref.shape[0], LANES):
        here = slice(first + tile, first + tile + LANES)
        block = slice(tile, tile + LANES)
        sums[...] = jnp.zeros_like(sums)
        sizes = sizes_ref[:, here]

        def fill(row, carry):
            cells = pl.ds(pl.multiple_of(row * SIDE, 16), SIDE)
            framed[pl.ds(frame_at(row, 0), SIDE)] = masked_ref[cells, here].astype(f32)
            grads = jnp.where(valid_row(row, sizes), grad_cells[cells, here].astype(f32), 0.0)
            framed_grad[pl.ds(frame_at(row, 0), SIDE)] = grads
            return carry

        lax.fori_loop(0, SIDE, fill, 0)

        def convolve(row, carry):
            cells = pl.ds(pl.multiple_of(row * SIDE, 16), SIDE)
            total = resid_cells[cells, here].astype(f32)
            grads = framed_grad[pl.ds(frame_at(row, 0), SIDE)]
            for row_step in range(KERNEL):
                for col_step in range(KERNEL):
                    tap = row_step * KERNEL + col_step
                    total = total + taps_ref[tap : tap + 1, here] * framed_grad[
                        pl.ds(frame_at(row + HALF - row_step, HALF - col_step), SIDE)
                    ]
                    shifted_in = framed[
                        pl.ds(frame_at(row + row_step - HALF, col_step - HALF), SIDE)
                    ]
                    sums[tap * 8 : tap * 8 + 8] += in_eights(grads * shifted_in)
            last = KERNEL * KERNEL * 8
            sums[last : last + 8] += in_eights(grads)
            field[cells] = jnp.where(valid_row(row, sizes), total, 0.0)
            return carry

        lax.fori_loop(0, SIDE, convolve, 0)
        for begin in range(0, CELLS, LANES):
            out_ref[block, begin : begin + LANES] = field[begin : begin + LANES].T
        for tap in range(KERNEL * KERNEL + 1):
            tap_grad_ref[tap : tap + 1, block] = jnp.sum(
                sums[tap * 8 : tap * 8 + 8], axis=0, keepdims=True
            )


def kernel_call(kernel, name, in_specs, out_shape, scratch_shapes=(), vmem=40):
    return pl.pallas_call(
        kernel,
        grid=(1,),
        in_specs=in_specs,
        out_specs=[whole(*out.shape) for out in out_shape],
        out_shape=out_shape,
        scratch_shapes=list(scratch_shapes),
        compiler_params=pltpu.CompilerParams(vmem_limit_bytes=vmem << 20),
        name=name,
    )


def conv_forward(hires, size_class, taps, bias, between):
    images, channels = hires.shape[:2]
    lanes = images * channels
    maps = hires.reshape(lanes, CELLS)
    sizes = jnp.repeat(size_class, channels)[None]
    lane_taps = jnp.tile(taps.astype(f32), (1, images))
    lane_bias = jnp.tile(bias.astype(f32)[None], (1, images))
    steps = size_class // BANDS * SIDE
    early = max(1, lanes // LANES * 2 // 3) * LANES
    bands = jax.ShapeDtypeStruct((images * BANDS, BAND_CELLS, channels), bf16)
    cells = jax.ShapeDtypeStruct((CELLS, lanes), bf16)
    early_cells = jax.ShapeDtypeStruct((CELLS, early), bf16)
    vectors = [whole(1, lanes), whole(KERNEL * KERNEL, lanes), whole(1, lanes)]
    scratch = [pltpu.VMEM((CELLS, LANES), f32), pltpu.VMEM((FRAME, LANES), f32)]
    given = (sizes, lane_taps, lane_bias)
    done = kernel_call(
        conv_forward_kernel,
        "depthwise_forward",
        vectors + [whole(early, CELLS)],
        [early_cells, early_cells],
        scratch,
    )(*given, maps)
    late = lanes - early
    late_maps = pl.BlockSpec((late, CELLS), lambda i: (early // late, 0))
    conv, masked_bands, masked = kernel_call(
        conv_forward_last_kernel,
        "depthwise_forward_last",
        [in_smem()] + vectors + [late_maps, whole(CELLS, early), whole(CELLS, early)],
        [bands, bands, cells],
        scratch + [pltpu.VMEM((CELLS, lanes), bf16)],
    )(steps, *given, maps, *between(done))
    return conv, masked_bands, (steps, sizes, lane_taps, masked)


def conv_backward(saved, grad_bands, resid_bands, between):
    steps, sizes, lane_taps, masked = saved
    images, lanes, taps = steps.shape[0], sizes.shape[1], KERNEL * KERNEL
    early = max(1, lanes // LANES * 2 // 3) * LANES
    args = [steps, sizes, lane_taps, masked, grad_bands, resid_bands]
    specs = [in_smem(), whole(1, lanes), whole(taps, lanes), whole(CELLS, lanes)]
    specs += [whole(*grad_bands.shape), whole(*resid_bands.shape)]
    tap_grads = []
    for first, count in ((0, early), (early, lanes - early)):
        index = first // count
        field, tap_grad = pl.pallas_call(
            partial(conv_backward_kernel, first=first),
            grid=(1,),
            in_specs=specs,
            out_specs=[
                pl.BlockSpec((count, CELLS), lambda i, index=index: (index, 0)),
                whole(taps + 1, count),
            ],
            out_shape=[
                jax.ShapeDtypeStruct((lanes, CELLS), f32),
                jax.ShapeDtypeStruct((taps + 1, count), f32),
            ],
            input_output_aliases={6: 0} if first else {},
            scratch_shapes=[
                pltpu.VMEM((FRAME, LANES), f32),
                pltpu.VMEM((FRAME, LANES), f32),
                pltpu.VMEM((CELLS, LANES), f32),
                pltpu.VMEM(((taps + 1) * 8, LANES), f32),
                pltpu.VMEM((CELLS, lanes), bf16),
                pltpu.VMEM((CELLS, lanes), bf16),
            ],
            compiler_params=pltpu.CompilerParams(vmem_limit_bytes=40 << 20),
            name="depthwise_backward",
        )(*args)
        tap_grads.append(tap_grad)
        if not first:
            field = between(field)
            args.append(field)
            specs = specs + [pl.BlockSpec(memory_space=pl.ANY)]
    tap_grads = jnp.concatenate(tap_grads, axis=1).reshape(taps + 1, images, -1)
    return field.reshape(images, -1, CELLS), jnp.sum(tap_grads, axis=1)


def shape_of(dtype, *shape):
    return jax.ShapeDtypeStruct(shape, dtype)


def blocks_of(arrays):
    return [whole(*array.shape) for array in arrays]


def split_rows(count):
    return next(rows for rows in (96, 64, 48, 32, 16) if count % rows == 0)


def conv_norm_kernel(blocks_ref, gain_ref, bias_ref, out_ref):
    parts, rows, channels = blocks_ref.shape
    width = parts * channels
    blocks = [blocks_ref[part].astype(f32) for part in range(parts)]
    mean = sum(jnp.sum(block, axis=1, keepdims=True) for block in blocks) / width
    blocks = [block - mean for block in blocks]
    variance = sum(jnp.sum(block * block, axis=1, keepdims=True) for block in blocks) / width
    scale = lax.rsqrt(variance + EPS_CONV)
    for part in range(parts):
        here = slice(part * channels, (part + 1) * channels)
        normed = blocks[part] * scale * gain_ref[:, here] + bias_ref[:, here]
        out_ref[:, here] = normed.astype(bf16)


def conv_norm_forward(blocks, gain, bias):
    parts, cells, channels = blocks.shape
    width, rows = parts * channels, split_rows(cells)
    return pl.pallas_call(
        conv_norm_kernel,
        grid=(cells // rows,),
        in_specs=[
            pl.BlockSpec((parts, rows, channels), lambda i: (0, i, 0)),
            whole(1, width),
            whole(1, width),
        ],
        out_specs=pl.BlockSpec((rows, width), lambda i: (i, 0)),
        out_shape=shape_of(bf16, cells, width),
        compiler_params=pltpu.CompilerParams(vmem_limit_bytes=32 << 20),
        name="conv_norm_forward",
    )(blocks, gain[None], bias[None])


def conv_norm_grad_kernel(blocks_ref, gain_ref, own_ref, other_ref, out_ref, sums_ref):
    parts, rows, channels = blocks_ref.shape
    width = parts * channels

    @pl.when(pl.program_id(0) == 0)
    def _():
        sums_ref[...] = jnp.zeros_like(sums_ref)

    blocks = [blocks_ref[part].astype(f32) for part in range(parts)]
    mean = sum(jnp.sum(block, axis=1, keepdims=True) for block in blocks) / width
    blocks = [block - mean for block in blocks]
    variance = sum(jnp.sum(block * block, axis=1, keepdims=True) for block in blocks) / width
    scale = lax.rsqrt(variance + EPS_CONV)
    grads, mean_grad, mean_both = [], 0.0, 0.0
    for part in range(parts):
        here = slice(part * channels, (part + 1) * channels)
        grad = own_ref[:, here].astype(f32) + other_ref[:, here].astype(f32)
        blocks[part] = blocks[part] * scale
        both = grad * blocks[part]
        sums_ref[0:1, here] += jnp.sum(both, axis=0, keepdims=True)
        sums_ref[1:2, here] += jnp.sum(grad, axis=0, keepdims=True)
        grads.append(grad * gain_ref[:, here])
        mean_grad += jnp.sum(grads[part], axis=1, keepdims=True)
        mean_both += jnp.sum(grads[part] * blocks[part], axis=1, keepdims=True)
    for part in range(parts):
        value = grads[part] - mean_grad / width - blocks[part] * (mean_both / width)
        out_ref[part] = (scale * value).astype(bf16)


def conv_norm_backward(blocks, gain, own, other):
    parts, cells, channels = blocks.shape
    width, rows = parts * channels, split_rows(cells)
    return pl.pallas_call(
        conv_norm_grad_kernel,
        grid=(cells // rows,),
        in_specs=[
            pl.BlockSpec((parts, rows, channels), lambda i: (0, i, 0)),
            whole(1, width),
            pl.BlockSpec((rows, width), lambda i: (i, 0)),
            pl.BlockSpec((rows, width), lambda i: (i, 0)),
        ],
        out_specs=[
            pl.BlockSpec((parts, rows, channels), lambda i: (0, i, 0)),
            whole(2, width),
        ],
        out_shape=[shape_of(bf16, parts, cells, channels), shape_of(f32, 2, width)],
        compiler_params=pltpu.CompilerParams(vmem_limit_bytes=32 << 20),
        name="conv_norm_backward",
    )(blocks, gain[None], own, other)


def dot_nt(left, right):
    return lax.dot_general(left, right, (((1,), (1,)), ((), ())), preferred_element_type=f32)


def dot_tn(left, right):
    return lax.dot_general(left, right, (((0,), (0,)), ((), ())), preferred_element_type=f32)


def head_parts(joined, head, share):
    return [
        joined[:, kind * share + head * HEAD_DIM : kind * share + (head + 1) * HEAD_DIM]
        for kind in range(3)
    ]


def softmax_rows(queries, keys):
    scores = dot_nt(queries, keys) * HEAD_DIM ** (-0.5)
    weights = jnp.exp(scores - jnp.max(scores, axis=1, keepdims=True))
    return weights / jnp.sum(weights, axis=1, keepdims=True)


def attention_kernel(*refs):
    inputs, (context_ref, joined_ref) = refs[:BANDS], refs[BANDS:]
    for band in range(BANDS):
        joined_ref[band * TOKENS : (band + 1) * TOKENS] = inputs[band][...]
    share = context_ref.shape[2]
    for head in range(share // HEAD_DIM):
        queries, keys, values = head_parts(joined_ref, head, share)
        probs = softmax_rows(queries, keys).astype(bf16)
        context = jnp.dot(probs, values, preferred_element_type=f32).astype(bf16)
        for band in range(BANDS):
            context_ref[band, :, head * HEAD_DIM : (head + 1) * HEAD_DIM] = context[
                band * TOKENS : (band + 1) * TOKENS
            ]


def attention(pieces):
    share = pieces[0].shape[1] // 3
    return kernel_call(
        attention_kernel,
        "attention_forward",
        blocks_of(pieces),
        [shape_of(bf16, BANDS, TOKENS, share), shape_of(bf16, BANDS * TOKENS, 3 * share)],
    )(*pieces)


def attention_grad_kernel(joined_ref, *refs):
    inputs, (out_ref, grad_ref, result) = refs[:BANDS], refs[BANDS:]
    for band in range(BANDS):
        grad_ref[band * TOKENS : (band + 1) * TOKENS] = inputs[band][...]
    share = grad_ref.shape[1]
    for head in range(share // HEAD_DIM):
        queries, keys, values = head_parts(joined_ref, head, share)
        grads = grad_ref[:, head * HEAD_DIM : (head + 1) * HEAD_DIM]
        probs = softmax_rows(queries, keys)
        grad_probs = dot_nt(grads, values)
        row_dot = jnp.sum(probs * grad_probs, axis=1, keepdims=True)
        grad_scores = (probs * (grad_probs - row_dot)).astype(bf16)
        scale = HEAD_DIM ** (-0.5)
        parts = (
            jnp.dot(grad_scores, keys, preferred_element_type=f32) * scale,
            dot_tn(grad_scores, queries) * scale,
            dot_tn(probs.astype(bf16), grads),
        )
        for kind, part in enumerate(parts):
            begin = kind * share + head * HEAD_DIM
            result[:, begin : begin + HEAD_DIM] = part.astype(bf16)
    for band in range(BANDS):
        out_ref[band] = result[band * TOKENS : (band + 1) * TOKENS]


def attention_grad(joined, pieces):
    share = pieces[0].shape[1]
    return kernel_call(
        attention_grad_kernel,
        "attention_backward",
        [whole(*joined.shape)] + blocks_of(pieces),
        [shape_of(bf16, BANDS, TOKENS, 3 * share)],
        [
            pltpu.VMEM((BANDS * TOKENS, share), bf16),
            pltpu.VMEM((BANDS * TOKENS, 3 * share), bf16),
        ],
    )(joined, *pieces)[0]


GRID_PITCH = GRID + 8
GRID_FRAME = (ROWS + 2) * GRID_PITCH + 8


def fill_frame(frame_ref, keep_ref, before_ref, inner_ref, after_ref):
    frame_ref[...] = jnp.zeros_like(frame_ref)
    inner = inner_ref[...].astype(f32)
    rows = [before_ref[...].astype(f32) * keep_ref[0].astype(f32)]
    rows += [inner[row * GRID : (row + 1) * GRID] for row in range(ROWS)]
    rows += [after_ref[...].astype(f32) * keep_ref[1].astype(f32)]
    for row, value in enumerate(rows):
        begin = row * GRID_PITCH + 8
        frame_ref[begin : begin + GRID] = value


def frame_row(frame_ref, row, col):
    begin = row * GRID_PITCH + 8 + col
    return frame_ref[begin : begin + GRID]


def vit_norm(value):
    mean = jnp.mean(value, axis=1, keepdims=True)
    centred = value - mean
    variance = jnp.mean(centred * centred, axis=1, keepdims=True)
    scale = lax.rsqrt(variance + EPS_VIT)
    return centred * scale, scale


def mix_kernel(
    keep_ref, before_ref, inner_ref, after_ref, taps_ref, vectors_ref, vit_ref, adapt_ref, mixed_ref, norm_ref, frame
):
    fill_frame(frame, keep_ref, before_ref, inner_ref, after_ref)
    bias, gate_tanh, gain, shift = (vectors_ref[i : i + 1] for i in range(4))
    for row in range(ROWS):
        total = jnp.zeros((GRID, D), f32) + bias
        for row_step in range(3):
            for col_step in range(3):
                tap = row_step * 3 + col_step
                total = total + taps_ref[tap : tap + 1] * frame_row(
                    frame, row + row_step, col_step - 1
                )
        adapt_ref[row * GRID : (row + 1) * GRID] = total
    mixed = vit_ref[...].astype(f32) + gate_tanh * adapt_ref[...]
    mixed_ref[...] = mixed
    norm_ref[...] = (vit_norm(mixed)[0] * gain + shift).astype(bf16)


def mix_forward(keep, before, inner, after, taps, vectors, vit_in):
    return kernel_call(
        mix_kernel,
        "mix_forward",
        [in_smem()] + blocks_of((before, inner, after, taps, vectors, vit_in)),
        [shape_of(f32, TOKENS, D), shape_of(f32, TOKENS, D), shape_of(bf16, TOKENS, D)],
        [pltpu.VMEM((GRID_FRAME, D), f32)],
    )(keep, before, inner, after, taps, vectors, vit_in)


def norm_grad(value, gain, grad):
    xhat, scale = vit_norm(value)
    gained = grad * gain
    back = (
        gained
        - jnp.mean(gained, axis=1, keepdims=True)
        - xhat * jnp.mean(gained * xhat, axis=1, keepdims=True)
    )
    return (
        scale * back,
        jnp.sum(grad * xhat, axis=0, keepdims=True),
        jnp.sum(grad, axis=0, keepdims=True),
    )


def mix_grad_kernel(vectors_ref, grad_ref, mixed_ref, resid_ref, adapt_ref, out_ref, low_ref, sums_ref):
    gate_tanh, gain = vectors_ref[1:2], vectors_ref[2:3]
    back, sums_ref[0:1], sums_ref[1:2] = norm_grad(mixed_ref[...], gain, grad_ref[...])
    vit_grad = resid_ref[...] + back
    out_ref[...] = vit_grad
    low = (gate_tanh * vit_grad).astype(bf16)
    low_ref[...] = low
    gate_sum = jnp.sum(vit_grad * adapt_ref[...], axis=0, keepdims=True)
    sums_ref[2:3] = gate_sum * (1.0 - gate_tanh * gate_tanh)
    sums_ref[3:4] = jnp.sum(low.astype(f32), axis=0, keepdims=True)


def mix_grad(vectors, grad_norm1, mixed, grad_resid, adapt_flat):
    args = (vectors, grad_norm1, mixed, grad_resid, adapt_flat)
    return kernel_call(
        mix_grad_kernel,
        "mix_backward",
        blocks_of(args),
        [shape_of(f32, TOKENS, D), shape_of(bf16, TOKENS, D), shape_of(f32, 4, D)],
    )(*args)


def adapt_grad_kernel(
    keep_ref, before_ref, inner_ref, after_ref, b_ref, i_ref, a_ref, taps_ref, low_ref, sums_ref, frame, frame_in
):
    fill_frame(frame, keep_ref, before_ref, inner_ref, after_ref)
    fill_frame(frame_in, keep_ref, b_ref, i_ref, a_ref)
    tap_sums = [jnp.zeros((GRID, D), f32) for tap in range(9)]
    bias_sum = jnp.zeros((GRID, D), f32)
    rows = []
    for row in range(ROWS):
        grads = frame_row(frame, row + 1, 0)
        total = jnp.zeros((GRID, D), f32)
        for row_step in range(3):
            for col_step in range(3):
                tap = row_step * 3 + col_step
                total = total + taps_ref[tap : tap + 1] * frame_row(
                    frame, row + 2 - row_step, 1 - col_step
                )
                tap_sums[tap] += grads * frame_row(frame_in, row + row_step, col_step - 1)
        rows.append(total)
    low = jnp.concatenate(rows, axis=0).astype(bf16)
    low_ref[...] = low
    for tap in range(9):
        sums_ref[tap : tap + 1] = jnp.sum(tap_sums[tap], axis=0, keepdims=True)
    sums_ref[9:10] = jnp.sum(low.astype(f32), axis=0, keepdims=True)


def adapt_grad(keep, grad_rims, input_rims, taps):
    args = (*grad_rims, *input_rims, taps)
    return kernel_call(
        adapt_grad_kernel,
        "adapter_backward",
        [in_smem()] + blocks_of(args),
        [shape_of(bf16, TOKENS, D), shape_of(f32, 10, D)],
        [pltpu.VMEM((GRID_FRAME, D), f32), pltpu.VMEM((GRID_FRAME, D), f32)],
    )(keep, *args)


def gelu_parts(hidden):
    below = 0.5 * (1.0 + lax.erf(hidden * (0.5**0.5)))
    slope = below + hidden * jnp.exp(-0.5 * hidden * hidden) * 0.3989422804014327
    return hidden * below, slope


def mlp_kernel(
    norm_ref, cot_ref, fc1_ref, bias_ref, fc2_ref, out_in, grad_in, out_ref, grad_ref, g1_ref, gb_ref, g2_ref
):
    @pl.when(pl.program_id(0) == 0)
    def _():
        out_ref[...] = out_in[...]
        grad_ref[...] = grad_in[...]

    norm, cot, fc1, fc2 = norm_ref[...], cot_ref[...], fc1_ref[...], fc2_ref[...]
    hidden = jnp.dot(norm, fc1, preferred_element_type=f32) + bias_ref[...]
    act, slope = gelu_parts(hidden)
    act = act.astype(bf16)
    out_ref[...] += jnp.dot(act, fc2, preferred_element_type=f32)
    grad_hidden = (slope * dot_nt(cot, fc2)).astype(bf16)
    g2_ref[...] = dot_tn(act, cot).astype(bf16)
    g1_ref[...] = dot_tn(norm, grad_hidden).astype(bf16)
    gb_ref[...] = jnp.sum(grad_hidden.astype(f32), axis=0, keepdims=True)
    grad_ref[...] += dot_nt(grad_hidden, fc1)


def mlp_piece(norm, cotangent, fc1, bias, fc2, out_so_far, grad_so_far):
    hidden = fc1.shape[1]
    step = next(size for size in (512, 256, 128) if hidden % size == 0)
    columns = pl.BlockSpec((D, step), lambda i: (0, i))
    down = pl.BlockSpec((step, D), lambda i: (i, 0))
    bias_block = pl.BlockSpec((1, step), lambda i: (0, i))
    tokens = whole(TOKENS, D)
    return pl.pallas_call(
        mlp_kernel,
        grid=(hidden // step,),
        in_specs=[tokens, tokens, columns, bias_block, down, tokens, tokens],
        out_specs=[tokens, tokens, columns, bias_block, down],
        out_shape=[
            shape_of(f32, TOKENS, D),
            shape_of(f32, TOKENS, D),
            shape_of(bf16, D, hidden),
            shape_of(f32, 1, hidden),
            shape_of(bf16, hidden, D),
        ],
        compiler_params=pltpu.CompilerParams(vmem_limit_bytes=40 << 20),
        name="mlp_piece",
    )(norm, cotangent, fc1, bias[None], fc2, out_so_far, grad_so_far)


def pick_columns(weight, parts, groups):
    rows, wide = weight.shape
    width = wide // parts // groups

    def kernel(index_ref, weight_ref, out_ref):
        for index in range(groups):

            @pl.when(index_ref[0] == index)
            def _():
                for part in range(parts):
                    begin = (part * groups + index) * width
                    out_ref[:, part * width : (part + 1) * width] = weight_ref[
                        :, begin : begin + width
                    ]

    return kernel_call(
        kernel, "pick_columns", [in_smem(), whole(rows, wide)], [shape_of(bf16, rows, wide // groups)]
    )(lax.axis_index(GRP)[None], weight)[0]


def place_columns(pieces, parts):
    groups = len(pieces)
    rows, narrow = pieces[0].shape
    width = narrow // parts

    def kernel(index_ref, *refs):
        inputs, out_ref = refs[:groups], refs[groups]
        for index in range(groups):

            @pl.when(index_ref[0] == index)
            def _():
                for place in range(groups):
                    for part in range(parts):
                        begin = (part * groups + (place ^ index)) * width
                        out_ref[:, begin : begin + width] = inputs[place][
                            :, part * width : (part + 1) * width
                        ].astype(f32)

    return kernel_call(
        kernel, "place_columns", [in_smem()] + blocks_of(pieces), [shape_of(f32, rows, narrow * groups)]
    )(lax.axis_index(GRP)[None], *pieces)[0]


def bundle_rows(vectors, parts):
    vectors = [vector.reshape(1, -1) for vector in vectors]
    length = sum(vector.shape[1] for vector in vectors) // parts

    def kernel(*refs):
        inputs, out_ref = refs[:-1], refs[-1]
        begin = 0
        for ref in inputs:
            size = ref.shape[1] // parts
            for part in range(parts):
                out_ref[part : part + 1, begin : begin + size] = ref[
                    :, part * size : (part + 1) * size
                ]
            begin += size

    rows = kernel_call(kernel, "bundle_rows", blocks_of(vectors), [shape_of(f32, parts, length)])(
        *vectors
    )[0]
    return rows.reshape(-1, LANES)


def joint_grads(norm, grad_pieces, context, out_pieces):
    part, count = out_pieces[0].shape[1], len(out_pieces)

    def kernel(norm_ref, context_ref, *refs):
        for place in range(count):
            grads, outs, result = refs[place], refs[count + place], refs[2 * count + place]
            result[:, : 3 * part] = dot_tn(norm_ref[...], grads[...]).astype(bf16)
            result[:, 3 * part :] = dot_tn(context_ref[...], outs[...]).astype(bf16)

    return kernel_call(
        kernel,
        "joint_grads",
        blocks_of((norm, context, *grad_pieces, *out_pieces)),
        [shape_of(bf16, D, 4 * part)] * count,
    )(norm, context, *grad_pieces, *out_pieces)


def side_by_side(vectors):
    vectors = [vector.reshape(1, -1) for vector in vectors]

    def kernel(*refs):
        begin = 0
        for ref in refs[:-1]:
            size = ref.shape[1]
            refs[-1][:, begin : begin + size] = ref[...].astype(f32)
            begin += size

    length = sum(vector.shape[1] for vector in vectors)
    joined = kernel_call(kernel, "side_by_side", blocks_of(vectors), [shape_of(f32, 1, length)])(
        *vectors
    )[0]
    return joined.reshape(-1, LANES)


def band_slices(cells, size_class):
    bands = []
    for image, image_cells in enumerate(cells):
        step = size_class[image] // BANDS * SIDE
        for band in range(BANDS):
            bands.append(lax.dynamic_slice_in_dim(image_cells, band * step, BAND_CELLS, 0))
    return jnp.stack(bands)


def pool_tables(size_class, mask_bands):
    sizes = jnp.repeat(size_class, BANDS)[:, None, None]
    out_ids = lax.broadcasted_iota(jnp.int32, (1, TOKENS, 1), 1)
    out_row, out_col = out_ids // GRID, out_ids % GRID
    cell_ids = lax.broadcasted_iota(jnp.int32, (1, 1, BAND_CELLS), 2)
    cell_row, cell_col = cell_ids // SIDE, cell_ids % SIDE
    row_hit = (out_row * sizes // GRID <= cell_row) & (
        cell_row < ((out_row + 1) * sizes + GRID - 1) // GRID
    )
    col_hit = (out_col * sizes // GRID <= cell_col) & (
        cell_col < ((out_col + 1) * sizes + GRID - 1) // GRID
    )
    return jnp.where(row_hit & col_hit, mask_bands[:, None, :], 0).astype(bf16)


def batched(left, right, left_dim, right_dim):
    return lax.dot_general(
        left, right, (((left_dim,), (right_dim,)), ((0,), (0,))), preferred_element_type=f32
    )


class Small(NamedTuple):
    ln1_gain: Any
    ln1_bias: Any
    qv_bias: Any
    out_bias: Any
    ln2_gain: Any
    ln2_bias: Any
    fc1_bias: Any
    fc2_bias: Any
    conv_gain: Any
    conv_bias: Any
    pw1_bias: Any
    pw2_bias: Any
    layer_scale: Any
    proj_bias: Any
    dw3_weight: Any
    dw3_bias: Any
    gate: Any


def body(
    vit_in,
    hires,
    size_class,
    pool_mask,
    cotangent,
    ln1_gain,
    ln1_bias,
    qkv_weight,
    qv_bias,
    out_weight,
    out_bias,
    ln2_gain,
    ln2_bias,
    fc1_weight,
    fc1_bias,
    fc2_weight,
    fc2_bias,
    dw7_weight,
    dw7_bias,
    conv_gain,
    conv_bias,
    pw1_weight,
    pw1_bias,
    pw2_weight,
    pw2_bias,
    layer_scale,
    proj_weight,
    proj_bias,
    dw3_weight,
    dw3_bias,
    gate,
):
    parts = lax.axis_size(CHAN)
    groups = lax.axis_size(GRP)
    chan_index = lax.axis_index(CHAN)
    band_index = chan_index % BANDS
    grp_index = lax.axis_index(GRP)
    width = hires.shape[1] * parts
    places = list(range(groups))
    part = D // groups

    along_chan = [(CHAN, bit) for bit in reversed(range(count_bits(CHAN)))]
    along_grp = [(GRP, bit) for bit in reversed(range(count_bits(GRP)))]
    conv_plan = along_chan + [step for step in along_grp if step[1] != PAIR]
    vit_plan = along_chan + along_grp

    rows = qkv_weight.shape[0]
    qkv_out_own = jnp.concatenate(
        [
            my_part(qkv_weight.reshape(rows, 3, groups, -1), 2).reshape(rows, -1),
            my_part(out_weight.reshape(rows, groups, -1), 1),
        ],
        axis=1,
    )
    qkv_out_flow = Flow(gather_crosswise(qkv_out_own, vit_plan))
    proj_flow = Flow(
        gather_crosswise(my_part(proj_weight.reshape(-1, groups, part), 1), vit_plan)
    )
    smalls = Small(
        ln1_gain,
        ln1_bias,
        qv_bias,
        out_bias,
        ln2_gain,
        ln2_bias,
        fc1_bias,
        fc2_bias,
        conv_gain,
        conv_bias,
        pw1_bias,
        pw2_bias,
        layer_scale,
        proj_bias,
        dw3_weight.reshape(-1),
        dw3_bias,
        gate,
    )
    small_flow = Flow(gather(side_by_side(smalls), along_chan))
    pw1_flow = Flow(gather(pick_columns(pw1_weight, parts, groups), conv_plan))
    flows = []

    def half_way(value):
        value = sync(value, small_flow)
        value, pw2_part = sync(
            (value, pw2_weight), small_flow, qkv_out_flow, proj_flow, pw1_flow
        )
        flows.append(Flow(gather(my_part(pw2_part.reshape(groups, -1, width), 0), conv_plan)))
        return value

    conv_bands, masked_bands, conv_saved = conv_forward(
        hires, size_class, dw7_weight, dw7_bias, half_way
    )
    pw2_flow = flows[0]
    conv_bands, masked_bands = sync(
        (conv_bands, masked_bands), qkv_out_flow, proj_flow
    )
    conv_recv = all_to_all(conv_bands)
    masked_bands, fc1_late, fc2_late = lax.optimization_barrier(
        (masked_bands, fc1_weight, fc2_weight)
    )
    fc1_own = my_part(fc1_late.reshape(rows, parts, groups, -1), 2).reshape(rows, -1)
    fc2_own = my_part(fc2_late.reshape(groups, -1, D), 0)
    tables = pool_tables(size_class, band_slices(pool_mask, size_class))
    all_counts = jnp.maximum(jnp.sum(tables.astype(f32), axis=2), 1.0)
    pooled_in = (batched(tables, masked_bands, 2, 1) / all_counts[:, :, None]).astype(bf16)
    table = lax.dynamic_index_in_dim(tables, chan_index, 0, keepdims=False)
    table_pair = jnp.stack([table, flip(table, GRP, PAIR)])
    count_raw = jnp.sum(table.astype(f32), axis=1)
    pool_count = jnp.maximum(count_raw, 1.0)[:, None]
    count_part = count_raw[:, None] / pool_count
    pooled_in = sync(pooled_in, pw1_flow, pw2_flow, qkv_out_flow, proj_flow, small_flow)
    small_full = small_flow.finish()[0].reshape(parts, -1)
    full, begin = [], 0
    for value in smalls:
        full.append(small_full[:, begin : begin + value.shape[0]].reshape(-1))
        begin += value.shape[0]
    small = Small(*full)
    dw3_taps = small.dw3_weight.reshape(parts, 9, -1).transpose(1, 0, 2).reshape(9, D)

    def hidden_bias(all_units, place):
        split = all_units.reshape(parts, groups, -1)
        return lax.dynamic_index_in_dim(split, grp_index ^ place, 1, keepdims=False).reshape(-1)

    normed_own = conv_norm_forward(conv_recv, small.conv_gain, small.conv_bias)
    normed_other = flip(normed_own, GRP, PAIR)
    normed_own = sync(normed_own, pw1_flow, qkv_out_flow, proj_flow)
    normed_own = sync(normed_own, pw2_flow)
    fc1_flow = Flow(gather_crosswise(fc1_own, vit_plan))
    fc2_flow = Flow(gather_crosswise(fc2_own, vit_plan))
    normed_other = sync(normed_other, fc1_flow, fc2_flow)
    normed_low = jnp.concatenate([normed_own, normed_other], axis=0)
    pw1 = pw1_flow.finish()
    conv_places = sorted(pw1)
    conv_act, conv_slope, branch = {}, {}, None
    for place in conv_places:
        hidden = matmul(normed_low, pw1[place]) + hidden_bias(small.pw1_bias, place)
        conv_act[place], conv_slope[place] = gelu_and_slope(hidden)
    conv_act, pooled_in = sync((conv_act, pooled_in), pw2_flow, fc1_flow, fc2_flow)
    pw2 = pw2_flow.finish()
    pooled_in = all_to_all(pooled_in)
    branch = matmul(conv_act[conv_places[0]], pw2[conv_places[0]])
    branch, pooled_in = sync((branch, pooled_in), fc1_flow, fc2_flow)
    for place in conv_places[1:]:
        branch = branch + matmul(conv_act[place], pw2[place])
    pooled_part = batched(
        table_pair, branch.astype(bf16).reshape(2, BAND_CELLS, width), 2, 1
    )
    pooled_other = flip(pooled_part[1].astype(bf16), GRP, PAIR)
    pooled_sum = pooled_part[0] + pooled_other.astype(f32)
    pooled_branch = pooled_sum / pool_count + small.pw2_bias * count_part
    pooled_in = pooled_in.transpose(1, 0, 2).reshape(TOKENS, width).astype(f32)
    pooled_low = (pooled_in + small.layer_scale * pooled_branch).astype(bf16)

    def in_columns(pieces):
        return jnp.concatenate(reorder([pieces[place] for place in places]), axis=1)

    def column_parts(value):
        return reorder(jnp.split(value, groups, axis=1))

    proj = proj_flow.finish()
    qkv_out = qkv_out_flow.finish()
    adapt = in_columns({place: matmul(pooled_low, proj[place]) for place in places})
    adapt_low = (adapt + small.proj_bias).astype(bf16)
    adapt_rims = (
        shifted(adapt_low[TOKENS - GRID :], CHAN, 1),
        adapt_low,
        shifted(adapt_low[:GRID], CHAN, -1),
    )
    keep = jnp.stack([band_index > 0, band_index < BANDS - 1]).astype(jnp.int32)
    gate_tanh = jnp.tanh(small.gate)
    vectors = jnp.stack([small.dw3_bias, gate_tanh, small.ln1_gain, small.ln1_bias])
    adapt_flat, mixed, norm1_low = mix_forward(keep, *adapt_rims, dw3_taps, vectors, vit_in)
    qv_split = small.qv_bias.reshape(2, groups, part)
    qkv_parts = []
    for place in places:
        biases = lax.dynamic_index_in_dim(qv_split, grp_index ^ place, 1, keepdims=False)
        bias = jnp.concatenate([biases[0], jnp.zeros((part,), f32), biases[1]])
        qkv_parts.append((matmul(norm1_low, qkv_out[place][:, : 3 * part]) + bias).astype(bf16))
    share = D // BANDS

    def band_shares(pieces):
        ratio = max(1, groups // BANDS)
        kinds = pieces[0].shape[1] // part
        if groups <= BANDS:
            cuts = []
            for piece in pieces:
                split = piece.reshape(TOKENS, kinds, BANDS // groups, share)
                cuts += [split[:, :, i].reshape(TOKENS, -1) for i in range(BANDS // groups)]
            return cuts
        joined = []
        for band in range(BANDS):
            own = [p.reshape(TOKENS, kinds, part) for p in pieces[band * ratio : (band + 1) * ratio]]
            joined.append(jnp.concatenate(own, axis=2).reshape(TOKENS, -1))
        return joined

    def grp_parts(shares):
        ratio = max(1, groups // BANDS)
        kinds = shares[0].shape[1] // share
        split = [s.reshape(TOKENS, kinds, share) for s in shares]
        if groups <= BANDS:
            each = BANDS // groups
            return [
                jnp.concatenate(split[i * each : (i + 1) * each], axis=2).reshape(TOKENS, -1)
                for i in range(groups)
            ]
        return [
            split[i // ratio][:, :, i % ratio * part : (i % ratio + 1) * part].reshape(TOKENS, -1)
            for i in range(groups)
        ]

    received = sync(band_exchange(band_shares(qkv_parts)), fc1_flow, fc2_flow)
    context, qkv_heads = attention(received)
    context_back = band_return(list(context))
    context_low = jnp.concatenate(reorder(grp_parts(context_back)), axis=1)
    attn = in_columns(
        {place: matmul(context_low, qkv_out[place][:, 3 * part :]) for place in places}
    )
    resid = mixed + attn + small.out_bias
    norm2, ln2_pullback = jax.vjp(norm_vit, resid, small.ln2_gain, small.ln2_bias)
    norm2_low = norm2.astype(bf16)
    vit_out = resid + small.fc2_bias
    grad_norm2 = jnp.zeros((TOKENS, D), f32)
    fc1, fc2 = fc1_flow.finish(), fc2_flow.finish()
    fc1_grads, fc2_grads, fc1_bias_grads = {}, {}, []
    for place in places:
        vit_out, grad_norm2, fc1_grads[place], bias_grad, fc2_grads[place] = mlp_piece(
            norm2_low,
            cotangent,
            fc1[place],
            hidden_bias(small.fc1_bias, place),
            fc2[place],
            vit_out,
            grad_norm2,
        )
        fc1_bias_grads.append(bias_grad.reshape(parts, -1))

    fc2_sum = Flow(scatter_and_spread(fc2_grads, vit_plan, crosswise_sum))
    fc1_sum = Flow(scatter_and_spread(fc1_grads, vit_plan, crosswise_sum))
    grads = SimpleNamespace(fc2_bias=column_sum(cotangent))

    def hidden_bias_grad(parts_rel):
        return jnp.stack(reorder(parts_rel), axis=1).reshape(-1)

    grads.fc1_bias = hidden_bias_grad(fc1_bias_grads)
    grad_resid_part, grads.ln2_gain, grads.ln2_bias = ln2_pullback(grad_norm2)
    grad_resid = cotangent.astype(f32) + grad_resid_part
    grad_attn_low = grad_resid.astype(bf16)
    grads.out_bias = column_sum(grad_attn_low)
    grad_attn_rel = column_parts(grad_attn_low)
    grad_context = sum(
        right_grad(grad_attn_rel[place], qkv_out[place][:, 3 * part :]) for place in places
    )
    context_grad_rel = band_shares(column_parts(grad_context.astype(bf16)))
    context_grads = sync(band_exchange(context_grad_rel), fc2_sum)
    qkv_grad_heads = attention_grad(qkv_heads, context_grads)
    qkv_grad_parts = grp_parts(band_return(list(qkv_grad_heads)))
    bias_rel = reorder([column_sum(g) for g in qkv_grad_parts])
    grads.qv_bias = jnp.concatenate(
        [g[:part] for g in bias_rel] + [g[2 * part :] for g in bias_rel]
    )
    grad_norm1 = sum(
        right_grad(qkv_grad_parts[place], qkv_out[place][:, : 3 * part]) for place in places
    )
    vit_grad, grad_conv3_low, mix_sums = mix_grad(vectors, grad_norm1, mixed, grad_resid, adapt_flat)
    grads.ln1_gain, grads.ln1_bias, grads.gate, grads.dw3_bias = mix_sums
    grad_rims = (
        shifted(grad_conv3_low[TOKENS - GRID :], CHAN, 1),
        grad_conv3_low,
        shifted(grad_conv3_low[:GRID], CHAN, -1),
    )
    grad_rims = sync(grad_rims, fc1_sum)
    joint = joint_grads(norm1_low, qkv_grad_parts, context_low, grad_attn_rel)
    joint_sum = Flow(
        scatter_and_spread(dict(enumerate(joint)), vit_plan, crosswise_sum)
    )
    grad_adapt_low, adapt_sums = adapt_grad(keep, grad_rims, adapt_rims, dw3_taps)
    grads.dw3_weight = adapt_sums[:9].reshape(9, parts, -1).transpose(1, 0, 2).reshape(-1)
    grads.proj_bias = adapt_sums[9]
    grad_adapt_rel = column_parts(grad_adapt_low)
    grad_pooled = sum(right_grad(grad_adapt_rel[place], proj[place]) for place in places)
    grad_pooled = grad_pooled.astype(bf16).astype(f32)
    grad_pool_sum = grad_pooled / pool_count
    scaled_own = (small.layer_scale * grad_pool_sum).astype(bf16)
    scaled_other = flip(scaled_own, GRP, PAIR)
    grads.layer_scale = jnp.sum(grad_pooled * pooled_branch, axis=0)
    grads.pw2_bias = small.layer_scale * jnp.sum(grad_pooled * count_part, axis=0)
    proj_sum = Flow(
        scatter_and_spread(
            {place: left_grad(pooled_low, grad_adapt_rel[place]) for place in places},
            vit_plan,
            crosswise_sum,
        )
    )
    scaled_other = sync(scaled_other, fc2_sum)
    grad_branch_low = (
        batched(table_pair, jnp.stack([scaled_own, scaled_other]), 1, 1)
        .astype(bf16)
        .reshape(2 * BAND_CELLS, width)
    )
    resid_back = all_to_all(
        grad_pool_sum.astype(bf16).reshape(TOKENS, parts, -1).transpose(1, 0, 2)
    )
    pw2_grads = {
        place: left_grad(conv_act[place], grad_branch_low) for place in reversed(conv_places)
    }
    grad_branch_low, pw2_grads = sync(
        (grad_branch_low, pw2_grads), fc1_sum, joint_sum, proj_sum
    )
    pw2_sum = Flow(scatter_and_spread(pw2_grads, conv_plan))
    grad_hidden, grad_normed_pair = {}, None
    for place in reversed(conv_places):
        grad_act = right_grad(grad_branch_low, pw2[place])
        grad_hidden[place] = (conv_slope[place].astype(f32) * grad_act).astype(bf16)
        if place == conv_places[-1]:
            grad_branch_low, grad_hidden = sync(
                (grad_branch_low, grad_hidden), pw2_sum, fc2_sum
            )
    for place in reversed(conv_places):
        product = right_grad(grad_hidden[place], pw1[place])
        grad_normed_pair = product if grad_normed_pair is None else grad_normed_pair + product
    grad_normed_pair, grad_hidden = sync(
        (grad_normed_pair.astype(bf16), grad_hidden), joint_sum, fc1_sum, fc2_sum
    )
    grad_normed_other = flip(grad_normed_pair[BAND_CELLS:], GRP, PAIR)
    pw1_grads = {}
    pw1_bias_grads = [jnp.zeros((parts, pw1_weight.shape[1] // parts // groups), f32)] * groups
    for place in reversed(conv_places):
        pw1_grads[place] = left_grad(normed_low, grad_hidden[place])
        pw1_bias_grads[place] = column_sum(grad_hidden[place]).reshape(parts, -1)
    pw1_sum = Flow(scatter_and_spread(pw1_grads, conv_plan))
    grads.pw1_bias = hidden_bias_grad(pw1_bias_grads)
    grad_normed_other, resid_back = sync(
        (grad_normed_other, resid_back), pw1_sum, pw2_sum, fc2_sum, fc1_sum, proj_sum
    )
    grad_conv_bands, norm_sums = conv_norm_backward(
        conv_recv, small.conv_gain, grad_normed_pair, grad_normed_other
    )
    grads.conv_gain, grads.conv_bias = norm_sums
    grad_conv_back = all_to_all(grad_conv_bands)
    resid_bands = batched(tables, resid_back, 1, 1).astype(bf16)
    others = (pw1_sum, pw2_sum, joint_sum, proj_sum, fc2_sum, fc1_sum)
    grad_conv_back, resid_bands = sync(
        (grad_conv_back, resid_bands), pw1_sum, pw2_sum, joint_sum, fc2_sum, fc1_sum
    )

    def half_way_back(value):
        value, bundle = lax.optimization_barrier(
            (sync(value, *others), bundle_rows(Small(**vars(grads)), parts))
        )
        flows.append(Flow(total_sum(bundle, vit_plan)))
        return value

    hires_grad, dw7_grads = conv_backward(conv_saved, grad_conv_back, resid_bands, half_way_back)
    bundle_sum = flows[1]
    hires_grad, dw7_grads = sync((hires_grad, dw7_grads), bundle_sum, *others)
    for axis, bit in along_grp:
        dw7_grads = dw7_grads + flip(dw7_grads, axis, bit)
    total = bundle_sum.finish().reshape(-1)
    sums, begin = [], 0
    for value in smalls:
        sums.append(total[begin : begin + value.shape[0]])
        begin += value.shape[0]
    sums = Small(*sums)

    grad_fc1 = place_columns(fc1_sum.finish(), parts)
    grad_fc2 = jnp.concatenate(reorder(fc2_sum.finish()), axis=0)
    grad_proj = jnp.concatenate(reorder(proj_sum.finish()), axis=1)
    joint_all = reorder(joint_sum.finish())
    grad_qkv = jnp.concatenate(
        [piece[:, kind * part : (kind + 1) * part] for kind in range(3) for piece in joint_all],
        axis=1,
    )
    grad_out = jnp.concatenate([piece[:, 3 * part :] for piece in joint_all], axis=1)
    grad_pw2 = jnp.concatenate(reorder(pw2_sum.finish()), axis=0)
    grad_pw1 = place_columns(pw1_sum.finish(), parts)
    return (
        vit_out,
        vit_grad,
        hires_grad,
        sums.ln1_gain,
        sums.ln1_bias,
        grad_qkv.astype(f32),
        sums.qv_bias,
        grad_out.astype(f32),
        sums.out_bias,
        sums.ln2_gain,
        sums.ln2_bias,
        grad_fc1,
        sums.fc1_bias,
        grad_fc2.astype(f32),
        sums.fc2_bias,
        dw7_grads[: KERNEL * KERNEL],
        dw7_grads[KERNEL * KERNEL],
        sums.conv_gain,
        sums.conv_bias,
        grad_pw1,
        sums.pw1_bias,
        grad_pw2.astype(f32),
        sums.pw2_bias,
        sums.layer_scale,
        grad_proj.astype(f32),
        sums.proj_bias,
        sums.dw3_weight.reshape(9, -1),
        sums.dw3_bias,
        sums.gate,
    )


def solution(mesh):
    in_specs = (
        P((GRP, CHAN), None),
        P(GRP, CHAN, None),
        P(GRP),
        P(GRP, None),
        P((GRP, CHAN), None),
        P(CHAN),
        P(CHAN),
        P(CHAN, None),
        P(CHAN),
        P(CHAN, None),
        P(CHAN),
        P(CHAN),
        P(CHAN),
        P(CHAN, None),
        P(CHAN),
        P(CHAN, None),
        P(CHAN),
        P(None, CHAN),
        P(CHAN),
        P(CHAN),
        P(CHAN),
        P(CHAN, None),
        P(CHAN),
        P(CHAN, None),
        P(CHAN),
        P(CHAN),
        P(CHAN, None),
        P(CHAN),
        P(None, CHAN),
        P(CHAN),
        P(CHAN),
    )
    out_specs = (
        P((GRP, CHAN), None),
        P((GRP, CHAN), None),
        P(GRP, CHAN, None),
        P(CHAN),
        P(CHAN),
        P(CHAN, None),
        P(CHAN),
        P(CHAN, None),
        P(CHAN),
        P(CHAN),
        P(CHAN),
        P(CHAN, None),
        P(CHAN),
        P(CHAN, None),
        P(CHAN),
        P(None, CHAN),
        P(CHAN),
        P(CHAN),
        P(CHAN),
        P(CHAN, None),
        P(CHAN),
        P(CHAN, None),
        P(CHAN),
        P(CHAN),
        P(CHAN, None),
        P(CHAN),
        P(None, CHAN),
        P(CHAN),
        P(CHAN),
    )
    return jax.shard_map(body, mesh=mesh, in_specs=in_specs, out_specs=out_specs, check_vma=False)
```
